256 devices in a mesh: dp: 64 (over y, x, z_hi), tensor: 4 (over z_lo, core).
Axes of the slice: x: 4, y: 4, z: 8 (z_hi: 4, z_lo: 2; z = z_hi * 2 + z_lo), core: 2. Of those that a mesh axis runs over, the one named last changes fastest.
Arguments:
- train_hidden: bfloat16 [512, 128, 14336], P('dp', None, 'tensor')
- train_grads: bfloat16 [512, 128, 4096], P('dp', None, 'tensor'), may hold values from -6 to 6
- train_ids: int32 [512, 128], P('dp'), may hold values from 0 to 128004, as said below
- query_hidden: bfloat16 [16, 1024, 14336], P(None, 'dp', 'tensor')
- query_grads: bfloat16 [16, 1024, 4096], P(None, 'dp', 'tensor'), may hold values from -6 to 6
- query_ids: int32 [16, 1024], P(None, 'dp'), may hold values from 0 to 128004, as said below
- proj_in: bfloat16 [14336, 64], P('tensor'), may hold values from -0.046875 to 0.046875
- proj_out: bfloat16 [4096, 64], P('tensor'), may hold values from -0.09375 to 0.09375
Outputs:
- scores: float32 [16, 512], P(None, ('dp', 'tensor'))
The draws below stay inside these ranges and needn't reach their ends.
Inputs may be any that keep to these rules, and one draw needn't show every extreme that they name: `train_ids`: id 128004 marks padding and appears only at the end of a sequence; the first 32 tokens of every training sequence are not padding; other ids lie below 128000. `query_ids`: id 128004 marks padding and appears only at the end of a query; the first 256 tokens of every query are not padding; other ids lie below 128000.
All inputs are finite; a program needn't handle non-finite values.
Results may differ from the reference program's by a relative error of at most 0.0003.
Values sent between devices are 32-bit elements; how exact they have to be, the bound alone decides.
A program may use at most 128 MiB of HBM per device.

```python
import math
import jax
import jax.numpy as jnp
from jax import lax

D = 4096
FF = 14336
RANK = 64
LEN = 128
QUERIES = 16
ITERS = 3
TRAIN = 512
QLEN = 1024
FEAT = 4096


def padded_ids(key, count, length):
    first, second = jax.random.split(key)
    lengths = jax.random.randint(first, (count, 1), length // 4, length + 1)
    tokens = jax.random.randint(second, (count, length), 0, 128000)
    places = jnp.arange(length)[None, :]
    return jnp.where(places < lengths, tokens, 128004).astype(jnp.int32)


def draw_train_ids(key, part):
    key = jax.random.fold_in(key, 11)
    return padded_ids(key, TRAIN, LEN)


def draw_query_ids(key, part):
    key = jax.random.fold_in(key, 12)
    return padded_ids(key, QUERIES, QLEN)


def draw_train_hidden(key, part):
    key = jax.random.fold_in(key, 21)
    first, second, third = jax.random.split(key, 3)
    rising = 3.0 ** (jnp.arange(TRAIN, dtype=jnp.float32) / TRAIN)
    rows = rising * jnp.exp(jax.random.uniform(first, (TRAIN,), jnp.float32, 0.0, math.log(3.4)))
    columns = jnp.exp(jax.random.uniform(second, (FF,), jnp.float32, math.log(0.5), math.log(2.0)))
    base = jax.random.normal(third, (TRAIN, LEN, FF), jnp.float32)
    return (base * rows[:, None, None] * columns[None, None, :]).astype(jnp.bfloat16)


def draw_query_hidden(key, part):
    key = jax.random.fold_in(key, 22)
    first, second, third = jax.random.split(key, 3)
    rising = 3.0 ** (jnp.arange(QLEN, dtype=jnp.float32) / QLEN)
    places = rising * jnp.exp(jax.random.uniform(first, (QLEN,), jnp.float32, 0.0, math.log(3.4)))
    columns = jnp.exp(jax.random.uniform(second, (FF,), jnp.float32, math.log(0.5), math.log(2.0)))
    base = jax.random.normal(third, (QUERIES, QLEN, FF), jnp.float32)
    return (base * places[None, :, None] * columns[None, None, :]).astype(jnp.bfloat16)


def steps_of(stream_key, shape, shards, smallest, largest):
    level, own = 1.0, jax.random.fold_in(stream_key, 6)
    for axis_at, parts in shards:
        heights = jnp.exp(jax.random.uniform(jax.random.fold_in(own, axis_at), (parts,), jnp.float32, smallest / len(shards), largest / len(shards)))
        level = level * jnp.repeat(heights, shape[axis_at] // parts).reshape([-1 if axis == axis_at else 1 for axis in range(len(shape))])
    return level


def scatter_about(rng, dims, width, most, cuts=(), kind=jnp.bfloat16):
    level = steps_of(rng, dims, cuts, -0.22, 0.18) if cuts else 1.0
    array = jax.random.normal(rng, dims, jnp.float32) * width * level
    return jnp.minimum(jnp.maximum(array, -most), most).astype(kind)


def setup_inputs(seed: int = 0) -> dict:
    keys = jax.random.split(jax.random.key(seed), 9)
    train_hidden = draw_train_hidden(jax.random.fold_in(keys[8], 71), 0)
    train_grads = scatter_about(keys[1], (TRAIN, LEN, D), 1.0, 6.0, ((0, 64), (2, 4)))
    train_ids = draw_train_ids(jax.random.fold_in(keys[8], 71), 0)
    query_hidden = draw_query_hidden(jax.random.fold_in(keys[8], 71), 0)
    query_grads = scatter_about(keys[4], (QUERIES, QLEN, D), 1.0, 6.0, ((1, 64), (2, 4)))
    query_ids = draw_query_ids(jax.random.fold_in(keys[8], 71), 0)
    proj_in = scatter_about(keys[6], (FF, RANK), FF ** -0.5, 0.046875, ((0, 4),))
    proj_out = scatter_about(keys[7], (D, RANK), D ** -0.5, 0.09375, ((0, 4),))
    return {"train_hidden": train_hidden, "train_grads": train_grads, "train_ids": train_ids, "query_hidden": query_hidden, "query_grads": query_grads, "query_ids": query_ids, "proj_in": proj_in, "proj_out": proj_out}


PAD_ID = 128004
DAMP = 0.1


def one_gradient(hidden, grads, ids, proj_in, proj_out):
    mask = (ids != PAD_ID).astype(jnp.float32)
    side_in = jnp.dot(hidden, proj_in, preferred_element_type=jnp.float32)
    side_out = jnp.dot(grads, proj_out, preferred_element_type=jnp.float32)
    outer = jnp.dot((side_in * mask[:, None]).T, side_out, precision=lax.Precision.HIGHEST)
    return outer.reshape(-1) / jnp.sum(mask)


def reference(train_hidden, train_grads, train_ids, query_hidden, query_grads, query_ids, proj_in, proj_out):
    def per_train(item):
        return one_gradient(item[0], item[1], item[2], proj_in, proj_out)

    examples = lax.map(per_train, (train_hidden, train_grads, train_ids))
    queries = lax.map(per_train, (query_hidden, query_grads, query_ids))
    trace = jnp.sum(examples * examples) / TRAIN
    damping = DAMP * trace / FEAT

    def apply(direction):
        inner = jnp.dot(direction, examples.T, precision=lax.Precision.HIGHEST)
        term = jnp.dot(inner, examples, precision=lax.Precision.HIGHEST)
        return direction + term / (TRAIN * damping)

    solved = jnp.zeros_like(queries)
    residual = queries
    direction = queries
    norm_now = jnp.sum(residual * residual, axis=1)
    for step in range(ITERS):
        image = apply(direction)
        alpha = norm_now / jnp.sum(direction * image, axis=1)
        solved = solved + alpha[:, None] * direction
        residual = residual - alpha[:, None] * image
        fresh = jnp.sum(residual * residual, axis=1)
        direction = residual + (fresh / norm_now)[:, None] * direction
        norm_now = fresh
    return jnp.dot(solved, examples.T, precision=lax.Precision.HIGHEST)
```

```python
import jax
import jax.numpy as jnp
from jax import lax
from jax.experimental import pallas as pl
from jax.experimental.pallas import tpu as pltpu
from jax.sharding import PartitionSpec as P

PAD_ID = 128004
DAMP = 0.1
TRAIN = 512
FEAT = 4096
MESH = pl.DeviceIdType.MESH
F32 = jnp.float32
BF16 = jnp.bfloat16


def kernel(
    th, tg, tids, qh, qg, qids, pin, pout, out,
    TH, TG, QH, QG, PIN, POUT, TIDS, QIDS, WI, WO,
    XQ, XT, RCQ, RCT, YQ, YT, RZQ, RZT,
    QPS, RQ1, CS, RC1, RQ2, ES, EO, EP, EH, EL, RB, SC, FR,
    hsem, cs, cr, zs, zr, q1s, q1r, q2s, q2r, es, er, fs, fr, rs, rr, osem, orem, lsem,
):
    dp = lax.axis_index("dp")
    tt = lax.axis_index("tensor")
    y = lax.div(dp, 16)
    x = lax.rem(lax.div(dp, 4), 4)
    zh = lax.rem(dp, 4)
    zl = lax.div(tt, 2)
    k = lax.rem(tt, 2)
    z = zh * 2 + zl
    col = y * 4 + x
    chip = dp * 2 + zl
    far = 1 - zl
    mate = (dp, zl * 2 + (1 - k))
    across = (dp, far * 2 + k)
    corner = (dp, far * 2 + (1 - k))

    loads = [
        pltpu.make_async_copy(pin, PIN, hsem.at[0]),
        pltpu.make_async_copy(qh, QH, hsem.at[1]),
        pltpu.make_async_copy(pout, POUT, hsem.at[2]),
        pltpu.make_async_copy(qg, QG, hsem.at[3]),
        pltpu.make_async_copy(qids, QIDS, hsem.at[4]),
        pltpu.make_async_copy(tids, TIDS, hsem.at[5]),
    ]
    firsts = []
    for unit in range(4):
        side = far if unit % 2 == 0 else zl
        first = (unit // 2) * 4 + side * 2
        firsts.append(first)
        pair = pl.ds(first, 2)
        loads.append(pltpu.make_async_copy(th.at[pair], TH.at[pair], hsem.at[6 + 2 * unit]))
        loads.append(pltpu.make_async_copy(tg.at[pair], TG.at[pair], hsem.at[7 + 2 * unit]))
    for load in loads:
        load.start()

    def chips(fn):
        def body(n, carry):
            ny = lax.rem(y + lax.rem(lax.div(n, 4), 4), 4)
            nx = lax.rem(x + lax.rem(n, 4), 4)
            nz = lax.rem(z + lax.div(n, 16), 8)
            there = ny * 4 + nx
            fn(there, (there * 4 + lax.div(nz, 2), lax.rem(nz, 2) * 2 + k))
            return carry

        lax.fori_loop(1, 128, body, 0)

    def plane(fn):
        def body(n, carry):
            there = lax.rem(y + lax.div(n, 4), 4) * 4 + lax.rem(x + lax.rem(n, 4), 4)
            fn(there, (there * 4 + zh, tt))
            return carry

        lax.fori_loop(1, 16, body, 0)

    barrier = pltpu.get_barrier_semaphore()

    def greet(there, device):
        pl.semaphore_signal(barrier, inc=1, device_id=device, device_id_type=MESH)

    chips(greet)
    greet(0, mate)
    greet(0, corner)

    def remote(src, dst, send, recv, device):
        return pltpu.make_async_remote_copy(
            src_ref=src, dst_ref=dst, send_sem=send, recv_sem=recv,
            device_id=device, device_id_type=MESH,
        )

    def drain(ref, sem):
        pltpu.make_async_copy(ref, ref, sem).wait()

    def project(hidden, grads):
        return jnp.dot(hidden, WI[...], preferred_element_type=F32) + jnp.dot(
            grads, WO[...], preferred_element_type=F32
        )

    loads[0].wait()
    WI[...] = jnp.concatenate([PIN[...], jnp.zeros_like(PIN)], axis=1)
    loads[2].wait()
    WO[...] = jnp.concatenate([jnp.zeros_like(POUT), POUT[...]], axis=1)

    loads[1].wait()
    loads[3].wait()
    XQ[...] = project(QH[...].reshape(256, -1), QG[...].reshape(256, -1)).reshape(2, 2, 64, 128)
    pl.semaphore_wait(barrier, 129)
    core_q = remote(XQ.at[:, 1 - k], RCQ, cs.at[0], cr.at[0], mate)
    core_q.start()

    def train_unit(unit):
        pair = pl.ds(firsts[unit], 2)
        loads[6 + 2 * unit].wait()
        loads[7 + 2 * unit].wait()
        XT[unit] = project(TH[pair].reshape(256, -1), TG[pair].reshape(256, -1)).reshape(2, 128, 128)
        copy = remote(XT.at[unit, 1 - k], RCT.at[unit], cs.at[1 + unit], cr.at[1 + unit], mate)
        copy.start()
        return copy

    def core_sum(unit, copy):
        copy.wait_recv()
        YT[unit] = XT[unit, k] + RCT[unit]

    def cross(chunk):
        copy = remote(YT.at[2 * chunk], RZT.at[chunk], zs.at[1 + chunk], zr.at[1 + chunk], across)
        copy.start()
        return copy

    lane = lax.broadcasted_iota(jnp.int32, (32, 128), 1)

    def pack(both):
        return jnp.where(lane < 64, pltpu.roll(both[0:32], 64, 1), both[32:64])

    core_0 = train_unit(0)

    core_q.wait_recv()
    YQ[...] = XQ[:, k] + RCQ[...]
    cross_q = remote(YQ.at[far], RZQ, zs.at[0], zr.at[0], across)
    cross_q.start()

    core_1 = train_unit(1)
    core_sum(0, core_0)
    cross_a = cross(0)

    cross_q.wait_recv()
    loads[4].wait()
    side = YQ[zl] + RZQ[...]
    mask = (QIDS[pl.ds(tt * 4, 4), :] != PAD_ID).astype(F32)
    CS[...] = jnp.broadcast_to(jnp.sum(mask, axis=1, keepdims=True), (4, 128))
    wide = jnp.concatenate([mask] * 4, axis=1)
    owner = lax.div(lax.broadcasted_iota(jnp.int32, (4, 64), 1), 16)
    wide = jnp.where(owner == lax.broadcasted_iota(jnp.int32, (4, 64), 0), wide, 0.0)
    turned = side.T[0:64]
    masked = jnp.concatenate([turned * wide[q : q + 1] for q in range(4)], axis=0)
    both = jnp.dot(masked, side, precision=lax.Precision.HIGHEST, preferred_element_type=F32)
    for q in range(4):
        QPS[pl.ds(q, 32, stride=4), :] = pack(both[q * 64 : q * 64 + 64])

    def send_q1(there, device):
        remote(QPS.at[pl.ds(there * 8, 8)], RQ1.at[col], q1s.at[0], q1r.at[0], device).start()
        remote(CS, RC1.at[col], q1s.at[1], q1r.at[1], device).start()

    plane(send_q1)
    own_q = pltpu.make_async_copy(QPS.at[pl.ds(col * 8, 8)], RQ1.at[col], lsem.at[0])
    own_q.start()
    RC1[col] = CS[...]

    core_2 = train_unit(2)
    core_sum(1, core_1)

    def example(chunk, copy):
        copy.wait_recv()
        seq = chunk * 4 + tt
        tokens = YT[2 * chunk + 1] + RZT[chunk]
        mask = (TIDS[pl.ds(seq, 1), :] != PAD_ID).astype(F32)
        both = jnp.dot(
            tokens.T[0:64] * mask, tokens,
            precision=lax.Precision.HIGHEST, preferred_element_type=F32,
        )
        ES[chunk] = pack(both) / jnp.sum(mask, axis=1, keepdims=True)
        spot = pl.ds(chip * 2, 2)

        def send(there, device):
            remote(
                ES.at[chunk, pl.ds(there * 2, 2)], EO.at[chunk, spot], es.at[chunk], er.at[chunk], device
            ).start()

        chips(send)
        own = pltpu.make_async_copy(
            ES.at[chunk, pl.ds(col * 2, 2)], EO.at[chunk, spot], lsem.at[1 + chunk]
        )
        own.start()
        return own

    core_3 = train_unit(3)
    core_sum(2, core_2)
    cross_b = cross(1)
    loads[5].wait()
    own_a = example(0, cross_a)
    core_sum(3, core_3)

    own_q.wait()
    drain(RQ1.at[pl.ds(0, 15)], q1r.at[0])
    drain(RC1.at[pl.ds(0, 15)], q1r.at[1])
    RQ2[zh, 0:8] = jnp.sum(RQ1[...], axis=0)
    RQ2[zh, 8:12] = jnp.sum(RC1[...], axis=0)
    for n in range(1, 4):
        device = (col * 4 + lax.rem(zh + n, 4), tt)
        remote(RQ2.at[zh], RQ2.at[zh], q2s, q2r, device).start()

    own_b = example(1, cross_b)

    def gathered(chunk, own):
        own.wait()
        drain(EO.at[chunk, pl.ds(0, 254)], er.at[chunk])
        copy = remote(EO.at[chunk], EP.at[chunk], fs.at[chunk], fr.at[chunk], mate)
        copy.start()
        return copy

    squares = jnp.zeros((128, 128), F32)

    def halves(ref, chunk, at, squares):
        for f in range(2):
            block = ref[chunk, pl.ds(f, 128, stride=2), :]
            squares = squares + block * block
            high = block.astype(BF16)
            EH[pl.ds(at, 128), f * 128 : f * 128 + 128] = high
            EL[pl.ds(at, 128), f * 128 : f * 128 + 128] = (block - high.astype(F32)).astype(BF16)
        return squares

    fwd_a = gathered(0, own_a)
    drain(RQ2.at[pl.ds(0, 3)], q2r)
    total = jnp.sum(RQ2[...], axis=0)
    queries = jnp.concatenate([total[0:4], total[4:8]], axis=1) / total[8:12, 0:1]
    squares = halves(EO, 0, 0, squares)
    fwd_a.wait_recv()
    squares = halves(EP, 0, 256, squares)
    fwd_b = gathered(1, own_b)
    squares = halves(EO, 1, 128, squares)
    fwd_b.wait_recv()
    squares = halves(EP, 1, 384, squares)

    def stacked(v):
        high = v.astype(BF16).astype(F32)
        return jnp.concatenate([high, v - high], axis=0).astype(BF16)

    def product(v, contract):
        v = stacked(v)
        dims = (((1,), (contract,)), ((), ()))
        whole = lax.dot_general(v, EH[...], dims, preferred_element_type=F32) + lax.dot_general(
            v, EL[...], dims, preferred_element_type=F32
        )
        return whole[0:4] + whole[4:8]

    spot = lax.broadcasted_iota(jnp.int32, (4, 128), 1)

    def share(step, partial_value, first, second):
        for b in range(4):
            RB[step, col, b] = partial_value[:, b * 128 : b * 128 + 128]
        RB[step, col, 4] = jnp.where(spot == 0, first, jnp.where(spot == 1, second, 0.0))

        def send(there, device):
            remote(RB.at[step, col], RB.at[step, col], rs.at[step], rr.at[step], device).start()

        plane(send)
        drain(RB.at[step, pl.ds(0, 15)], rr.at[step])
        whole = jnp.sum(RB[step], axis=0)
        return (
            jnp.concatenate([whole[b] for b in range(4)], axis=1),
            whole[4][:, 0:1],
            whole[4][:, 1:2],
        )

    def rowsum(v):
        return jnp.sum(v, axis=1, keepdims=True)

    residual = direction = queries
    trace = jnp.sum(jnp.sum(squares, axis=0, keepdims=True), axis=1, keepdims=True)
    seen, norm_now, trace = share(0, product(residual, 1), rowsum(residual * residual), trace)
    scale = TRAIN * (DAMP * (trace / TRAIN) / FEAT)
    length = norm_now
    scores = None
    for step in range(3):
        alpha = norm_now / (length + rowsum(seen * seen) / scale)
        scores = alpha * seen if step == 0 else scores + alpha * seen
        if step == 2:
            break
        image = direction + product(seen, 0) / scale
        residual = residual - alpha * image
        fresh_seen, fresh, along = share(
            step + 1, product(residual, 1), rowsum(residual * residual), rowsum(residual * direction)
        )
        beta = fresh / norm_now
        seen = fresh_seen + beta * seen
        length = fresh + 2.0 * beta * along + beta * beta * length
        direction = residual + beta * direction
        norm_now = fresh

    for chunk in range(2):
        for h in range(2):
            b = h * 2 + chunk
            SC[chunk, h] = scores[:, b * 128 : b * 128 + 128]
    for n, (oz, ok, device) in enumerate(((zl, 1 - k, mate), (far, k, across), (far, 1 - k, corner))):
        for p in range(2):
            remote(
                SC.at[oz, lax.rem(p + k, 2)], FR.at[p, tt], osem.at[n], orem.at[n * 2 + p], device
            ).start()
    for p in range(2):
        FR[p, tt] = SC[zl, lax.rem(p + k, 2)]
    for n in range(6):
        drain(FR.at[0, 0], orem.at[n])
    place = lax.broadcasted_iota(jnp.int32, (4, 4, 128), 2) == dp * 2 + k
    left = jnp.sum(jnp.where(place, FR[0], 0.0), axis=2, keepdims=True)
    right = jnp.sum(jnp.where(place, FR[1], 0.0), axis=2, keepdims=True)
    out[...] = jnp.where(lax.broadcasted_iota(jnp.int32, (4, 4, 2), 2) == 0, left, right)

    core_q.wait_send()
    cross_q.wait_send()
    for copy in (core_0, core_1, core_2, core_3, cross_a, cross_b, fwd_a, fwd_b):
        copy.wait_send()
    drain(RQ1.at[pl.ds(0, 15)], q1s.at[0])
    drain(RC1.at[pl.ds(0, 15)], q1s.at[1])
    drain(RQ2.at[pl.ds(0, 3)], q2s)
    for chunk in range(2):
        drain(EO.at[chunk, pl.ds(0, 254)], es.at[chunk])
    for step in range(3):
        drain(RB.at[step, pl.ds(0, 15)], rs.at[step])
    for n in range(3):
        drain(FR.at[0, pl.ds(0, 2)], osem.at[n])


def per_device(th, tg, tids, qh, qg, qids, pin, pout):
    V = pltpu.VMEM
    D = pltpu.SemaphoreType.DMA
    scores = pl.pallas_call(
        kernel,
        out_shape=jax.ShapeDtypeStruct((4, 4, 2), F32),
        in_specs=[pl.BlockSpec(memory_space=pl.ANY)] * 8,
        out_specs=pl.BlockSpec(memory_space=pltpu.VMEM),
        scratch_shapes=[
            V(th.shape, BF16), V(tg.shape, BF16), V(qh.shape, BF16), V(qg.shape, BF16),
            V(pin.shape, BF16), V(pout.shape, BF16), V(tids.shape, jnp.int32), V(qids.shape, jnp.int32),
            V((pin.shape[0], 128), BF16), V((pout.shape[0], 128), BF16),
            V((2, 2, 64, 128), F32), V((4, 2, 128, 128), F32),
            V((2, 64, 128), F32), V((4, 128, 128), F32),
            V((2, 64, 128), F32), V((4, 128, 128), F32),
            V((64, 128), F32), V((2, 128, 128), F32),
            V((128, 128), F32), V((16, 8, 128), F32),
            V((4, 128), F32), V((16, 4, 128), F32),
            V((4, 12, 128), F32),
            V((2, 32, 128), F32), V((2, 256, 128), F32), V((2, 256, 128), F32),
            V((512, 256), BF16), V((512, 256), BF16),
            V((3, 16, 5, 4, 128), F32),
            V((2, 2, 4, 128), F32), V((2, 4, 4, 128), F32),
            D((14,)), D((5,)), D((5,)), D((3,)), D((3,)), D((2,)), D((2,)), D, D,
            D((2,)), D((2,)), D((2,)), D((2,)), D((3,)), D((3,)), D((3,)), D((6,)), D((3,)),
        ],
        compiler_params=pltpu.CompilerParams(
            collective_id=0, has_side_effects=True, vmem_limit_bytes=56 * 1024 * 1024
        ),
        cost_estimate=pl.CostEstimate(flops=10**9, bytes_accessed=13 * 10**6, transcendentals=0),
    )(th, tg, tids, qh, qg, qids, pin, pout)
    return scores.reshape(16, 2)


def solution(mesh):
    return jax.shard_map(
        per_device,
        mesh=mesh,
        in_specs=(
            P("dp", None, "tensor"),
            P("dp", None, "tensor"),
            P("dp", None),
            P(None, "dp", "tensor"),
            P(None, "dp", "tensor"),
            P(None, "dp"),
            P("tensor", None),
            P("tensor", None),
        ),
        out_specs=P(None, ("dp", "tensor")),
        check_vma=False,
    )
```

```python
import jax
import jax.numpy as jnp
from jax import lax
from jax.experimental import pallas as pl
from jax.experimental.pallas import tpu as pltpu
from jax.sharding import PartitionSpec as P

PAD_ID = 128004
DAMP = 0.1
TRAIN = 512
FEAT = 4096
MESH = pl.DeviceIdType.MESH
F32 = jnp.float32
BF16 = jnp.bfloat16


SLOT = (0, 1, 3, 5, 7, 6, 4, 2)


def kernel(
    th, tg, tids, qh, qg, qids, pin, pout, out,
    TH, TG, QH, QG, TIDS, QIDS, WI, WO,
    XQ, XT, RCQ, RCT, YQ, YT, RZQ, RZT,
    QPS, RQ1, CS, RC1, RQ2, ES, EO, EP, EH, EL, RB, SC, FR,
    hsem, cs, cr, zs, zr, q1s, q1r, q2s, q2r, es, er, fs, fr, rs, rr, osem, orem, lsem, inside,
):
    dp = lax.axis_index("dp")
    tt = lax.axis_index("tensor")
    y = lax.div(dp, 16)
    x = lax.rem(lax.div(dp, 4), 4)
    zh = lax.rem(dp, 4)
    zl = lax.div(tt, 2)
    k = lax.rem(tt, 2)
    z = zh * 2 + zl
    col = y * 4 + x
    far = 1 - zl
    mate = (dp, zl * 2 + (1 - k))
    across = (dp, far * 2 + k)
    corner = (dp, far * 2 + (1 - k))

    def column(n):
        m = lax.rem(n + 10, 16)
        return lax.rem(y + lax.div(m, 4), 4) * 4 + lax.rem(x + lax.rem(m, 4), 4)

    def level(there, step):
        nz = lax.rem(z + step, 8)
        return (there * 4 + lax.div(nz, 2), lax.rem(nz, 2) * 2 + k)

    def plane(fn):
        def body(n, carry):
            there = column(n)
            fn(there, (there * 4 + zh, tt))
            return carry

        lax.fori_loop(0, 6, body, 0)
        lax.fori_loop(7, 16, body, 0)

    barrier = pltpu.get_barrier_semaphore()

    def greet(device):
        pl.semaphore_signal(barrier, inc=1, device_id=device, device_id_type=MESH)

    plane(lambda there, device: greet(device))
    for step in range(1, 8):
        greet(level(col, step))
    greet(mate)
    greet(corner)

    loads = [
        pltpu.make_async_copy(pin, WI.at[0:64], hsem.at[0]),
        pltpu.make_async_copy(qh, QH, hsem.at[1]),
        pltpu.make_async_copy(pout, WO.at[64:128], hsem.at[2]),
        pltpu.make_async_copy(qg, QG, hsem.at[3]),
        pltpu.make_async_copy(qids, QIDS, hsem.at[4]),
        pltpu.make_async_copy(tids, TIDS, hsem.at[5]),
    ]
    for unit in range(4):
        pair = pl.ds((unit % 2) * 4 + (far if unit < 2 else zl) * 2, 2)
        loads.append(pltpu.make_async_copy(th.at[pair], TH.at[unit], hsem.at[6 + 2 * unit]))
        loads.append(pltpu.make_async_copy(tg.at[pair], TG.at[unit], hsem.at[7 + 2 * unit]))
    for load in loads:
        load.start()

    def remote(src, dst, send, recv, device):
        return pltpu.make_async_remote_copy(
            src_ref=src, dst_ref=dst, send_sem=send, recv_sem=recv,
            device_id=device, device_id_type=MESH,
        )

    def drain(ref, sem):
        pltpu.make_async_copy(ref, ref, sem).wait()

    def project(hidden, grads):
        dims = (((1,), (1,)), ((), ()))
        return lax.dot_general(hidden, WI[...], dims, preferred_element_type=F32) + lax.dot_general(
            grads, WO[...], dims, preferred_element_type=F32
        )

    WI[64:128] = jnp.zeros_like(WI[64:128])
    WO[0:64] = jnp.zeros_like(WO[0:64])
    for n in range(4):
        loads[n].wait()
    for half in range(2):
        rows = slice(half * 8, half * 8 + 8)
        XQ[half] = project(QH[rows].reshape(128, -1), QG[rows].reshape(128, -1)).reshape(2, 64, 128)
    for unit in range(4):
        loads[6 + 2 * unit].wait()
        loads[7 + 2 * unit].wait()
        for half in range(2):
            XT[unit, half] = project(TH[unit, half], TG[unit, half])

    pl.semaphore_wait(barrier, 24)
    core = [remote(XT.at[u, 1 - k], RCT.at[u], cs.at[u], cr.at[u], mate) for u in range(4)]
    core_q = remote(XQ.at[:, 1 - k], RCQ, cs.at[4], cr.at[4], mate)
    for copy in core[:2] + [core_q] + core[2:]:
        copy.start()
    for step in range(1, 8):
        pl.semaphore_signal(inside, inc=1, device_id=level(col, step), device_id_type=MESH)

    cross = []
    for u in range(2):
        core[u].wait_recv()
        YT[u] = XT[u, k] + RCT[u]
        copy = remote(YT.at[u], RZT.at[u], zs.at[u], zr.at[u], across)
        copy.start()
        cross.append(copy)
    core_q.wait_recv()
    YQ[...] = XQ[:, k] + RCQ[...]
    cross_q = remote(YQ.at[far], RZQ, zs.at[2], zr.at[2], across)
    cross_q.start()
    for u in range(2, 4):
        core[u].wait_recv()
        YT[u] = XT[u, k] + RCT[u]

    lane = lax.broadcasted_iota(jnp.int32, (32, 128), 1)

    def pack(both):
        return jnp.where(lane < 64, pltpu.roll(both[0:32], 64, 1), both[32:64])

    def send_features(chunk, there, steps):
        for step in steps:
            slot = SLOT[step]
            remote(
                ES.at[chunk, pl.ds(there * 2, 2)], EO.at[slot, pl.ds(col * 4 + chunk * 2, 2)],
                es.at[slot], er.at[slot], level(there, step),
            ).start()

    loads[5].wait()
    owns = []
    for chunk in range(2):
        cross[chunk].wait_recv()
        tokens = YT[2 + chunk] + RZT[chunk]
        mask = (TIDS[pl.ds(chunk * 4 + tt, 1), :] != PAD_ID).astype(F32)
        both = jnp.dot(
            tokens.T[0:64] * mask, tokens,
            precision=lax.Precision.HIGHEST, preferred_element_type=F32,
        )
        packed = pack(both) / jnp.sum(mask, axis=1, keepdims=True)
        for f in range(2):
            ES[chunk, pl.ds(f, 16, stride=2), :] = packed[f * 16 : f * 16 + 16]
        if chunk == 0:
            pl.semaphore_wait(inside, 7)

        def features(n, carry, chunk=chunk):
            send_features(chunk, column(n), (4, 5, 3, 6, 2, 7, 1, 0))
            return carry

        lax.fori_loop(0, 6, features, 0)
        lax.fori_loop(7, 16, features, 0)
        send_features(chunk, col, (4, 5, 3, 6, 2, 7, 1))
        own = pltpu.make_async_copy(
            ES.at[chunk, pl.ds(col * 2, 2)], EO.at[0, pl.ds(col * 4 + chunk * 2, 2)], lsem.at[1 + chunk]
        )
        own.start()
        owns.append(own)

    loads[4].wait()
    cross_q.wait_recv()
    side = YQ[zl] + RZQ[...]
    mask = (QIDS[pl.ds(tt * 4, 4), :] != PAD_ID).astype(F32)
    CS[...] = jnp.broadcast_to(jnp.sum(mask, axis=1, keepdims=True), (4, 128))
    wide = jnp.concatenate([mask] * 4, axis=1)
    owner = lax.div(lax.broadcasted_iota(jnp.int32, (4, 64), 1), 16)
    wide = jnp.where(owner == lax.broadcasted_iota(jnp.int32, (4, 64), 0), wide, 0.0)
    turned = side.T[0:64]
    masked = jnp.concatenate([turned * wide[q : q + 1] for q in range(4)], axis=0)
    both = jnp.dot(masked, side, precision=lax.Precision.HIGHEST, preferred_element_type=F32)
    for q in range(4):
        packed = pack(both[q * 64 : q * 64 + 64])
        for f in range(2):
            QPS[pl.ds(f * 4 + q, 16, stride=8), :] = packed[f * 16 : f * 16 + 16]

    def send_q1(there, device):
        remote(QPS.at[pl.ds(there * 8, 8)], RQ1.at[col], q1s.at[0], q1r.at[0], device).start()
        remote(CS, RC1.at[col], q1s.at[1], q1r.at[1], device).start()

    plane(send_q1)
    own_q = pltpu.make_async_copy(QPS.at[pl.ds(col * 8, 8)], RQ1.at[col], lsem.at[0])
    own_q.start()
    RC1[col] = CS[...]

    own_q.wait()
    drain(RQ1.at[pl.ds(0, 15)], q1r.at[0])
    drain(RC1.at[pl.ds(0, 15)], q1r.at[1])
    RQ2[zh, 0:8] = jnp.sum(RQ1[...], axis=0)
    RQ2[zh, 8:12] = jnp.sum(RC1[...], axis=0)
    for n in range(1, 4):
        device = (col * 4 + lax.rem(zh + n, 4), tt)
        remote(RQ2.at[zh], RQ2.at[zh], q2s, q2r, device).start()

    squares = jnp.zeros((16, 128), F32)

    def halves(ref, slot, at, squares):
        for part in range(4):
            chunk, f = part // 2, part % 2
            block = ref[slot, pl.ds(part, 16, stride=4), :]
            squares = squares + block * block
            high = block.astype(BF16)
            rows = slice(at + slot * 32 + chunk * 16, at + slot * 32 + chunk * 16 + 16)
            EH[rows, f * 128 : f * 128 + 128] = high
            EL[rows, f * 128 : f * 128 + 128] = (block - high.astype(F32)).astype(BF16)
        return squares

    for own in owns:
        own.wait()
    forwards = []
    for slot in range(8):
        drain(EO.at[slot, pl.ds(0, 60 if slot == 0 else 64)], er.at[slot])
        copy = remote(EO.at[slot], EP.at[slot], fs.at[slot], fr.at[slot], mate)
        copy.start()
        forwards.append(copy)
        squares = halves(EO, slot, 0, squares)
    for slot in range(8):
        forwards[slot].wait_recv()
        squares = halves(EP, slot, 256, squares)

    drain(RQ2.at[pl.ds(0, 3)], q2r)
    total = jnp.sum(RQ2[...], axis=0)
    queries = jnp.concatenate([total[0:4], total[4:8]], axis=1) / total[8:12, 0:1]

    def stacked(v):
        high = v.astype(BF16).astype(F32)
        return jnp.concatenate([high, v - high], axis=0).astype(BF16)

    def product(v, contract):
        v = stacked(v)
        dims = (((1,), (contract,)), ((), ()))
        whole = lax.dot_general(v, EH[...], dims, preferred_element_type=F32) + lax.dot_general(
            v, EL[...], dims, preferred_element_type=F32
        )
        return whole[0:4] + whole[4:8]

    spot = lax.broadcasted_iota(jnp.int32, (4, 128), 1)

    def share(step, partial_value, first, second):
        for b in range(4):
            RB[step, col, b] = partial_value[:, b * 128 : b * 128 + 128]
        RB[step, col, 4] = jnp.where(spot == 0, first, jnp.where(spot == 1, second, 0.0))

        def send(there, device):
            remote(RB.at[step, col], RB.at[step, col], rs.at[step], rr.at[step], device).start()

        plane(send)
        drain(RB.at[step, pl.ds(0, 15)], rr.at[step])
        whole = jnp.sum(RB[step], axis=0)
        return (
            jnp.concatenate([whole[b] for b in range(4)], axis=1),
            whole[4][:, 0:1],
            whole[4][:, 1:2],
        )

    def rowsum(v):
        return jnp.sum(v, axis=1, keepdims=True)

    residual = direction = queries
    trace = jnp.sum(jnp.sum(squares, axis=0, keepdims=True), axis=1, keepdims=True)
    seen, norm_now, trace = share(0, product(residual, 1), rowsum(residual * residual), trace)
    scale = TRAIN * (DAMP * (trace / TRAIN) / FEAT)
    length = norm_now
    scores = None
    for step in range(3):
        alpha = norm_now / (length + rowsum(seen * seen) / scale)
        scores = alpha * seen if step == 0 else scores + alpha * seen
        if step == 2:
            break
        image = direction + product(seen, 0) / scale
        residual = residual - alpha * image
        fresh_seen, fresh, along = share(
            step + 1, product(residual, 1), rowsum(residual * residual), rowsum(residual * direction)
        )
        beta = fresh / norm_now
        seen = fresh_seen + beta * seen
        length = fresh + 2.0 * beta * along + beta * beta * length
        direction = residual + beta * direction
        norm_now = fresh

    for h in range(2):
        SC[h] = scores[:, h * 256 : h * 256 + 128]
    for n, device in enumerate((mate, across, corner)):
        for p in range(2):
            remote(
                SC.at[lax.rem(p + k, 2)], FR.at[p, tt], osem.at[n], orem.at[n * 2 + p], device
            ).start()
    for p in range(2):
        FR[p, tt] = SC[lax.rem(p + k, 2)]
    for n in range(6):
        drain(FR.at[0, 0], orem.at[n])
    own = zl * 16 + col
    group = lax.broadcasted_iota(jnp.int32, (4, 4, 128), 0)
    place = jnp.where(group < 2, k * 64, (1 - k) * 32) + own
    place = lax.broadcasted_iota(jnp.int32, (4, 4, 128), 2) == place
    left = jnp.sum(jnp.where(place, FR[0], 0.0), axis=2, keepdims=True)
    right = jnp.sum(jnp.where(place, FR[1], 0.0), axis=2, keepdims=True)
    out[...] = jnp.where(lax.broadcasted_iota(jnp.int32, (4, 4, 2), 2) == 0, left, right)

    core_q.wait_send()
    cross_q.wait_send()
    for copy in core + cross + forwards:
        copy.wait_send()
    drain(RQ1.at[pl.ds(0, 15)], q1s.at[0])
    drain(RC1.at[pl.ds(0, 15)], q1s.at[1])
    drain(RQ2.at[pl.ds(0, 3)], q2s)
    for slot in range(8):
        drain(EO.at[slot, pl.ds(0, 60 if slot == 0 else 64)], es.at[slot])
    for step in range(3):
        drain(RB.at[step, pl.ds(0, 15)], rs.at[step])
    for n in range(3):
        drain(FR.at[0, pl.ds(0, 2)], osem.at[n])


def per_device(th, tg, tids, qh, qg, qids, pin, pout):
    V = pltpu.VMEM
    D = pltpu.SemaphoreType.DMA
    scores = pl.pallas_call(
        kernel,
        out_shape=jax.ShapeDtypeStruct((4, 4, 2), F32),
        in_specs=[pl.BlockSpec(memory_space=pl.ANY)] * 8,
        out_specs=pl.BlockSpec(memory_space=pltpu.VMEM),
        scratch_shapes=[
            V((4, 2) + th.shape[1:], BF16), V((4, 2) + tg.shape[1:], BF16), V(qh.shape, BF16), V(qg.shape, BF16),
            V(tids.shape, jnp.int32), V(qids.shape, jnp.int32),
            V((128, pin.shape[0]), BF16), V((128, pout.shape[0]), BF16),
            V((2, 2, 64, 128), F32), V((4, 2, 128, 128), F32),
            V((2, 64, 128), F32), V((4, 128, 128), F32),
            V((2, 64, 128), F32), V((4, 128, 128), F32),
            V((64, 128), F32), V((2, 128, 128), F32),
            V((128, 128), F32), V((16, 8, 128), F32),
            V((4, 128), F32), V((16, 4, 128), F32),
            V((4, 12, 128), F32),
            V((2, 32, 128), F32), V((8, 64, 128), F32), V((8, 64, 128), F32),
            V((512, 256), BF16), V((512, 256), BF16),
            V((3, 16, 5, 4, 128), F32),
            V((2, 4, 128), F32), V((2, 4, 4, 128), F32),
            D((14,)), D((5,)), D((5,)), D((3,)), D((3,)), D((2,)), D((2,)), D, D,
            D((8,)), D((8,)), D((8,)), D((8,)), D((3,)), D((3,)), D((3,)), D((6,)), D((3,)),
            pltpu.SemaphoreType.REGULAR,
        ],
        compiler_params=pltpu.CompilerParams(
            collective_id=0, has_side_effects=True, vmem_limit_bytes=56 * 1024 * 1024
        ),
        cost_estimate=pl.CostEstimate(flops=10**9, bytes_accessed=13 * 10**6, transcendentals=0),
    )(th, tg, tids, qh, qg, qids, pin.T, pout.T)
    return scores.reshape(16, 2)


def solution(mesh):
    return jax.shard_map(
        per_device,
        mesh=mesh,
        in_specs=(
            P("dp", None, "tensor"),
            P("dp", None, "tensor"),
            P("dp", None),
            P(None, "dp", "tensor"),
            P(None, "dp", "tensor"),
            P(None, "dp"),
            P("tensor", None),
            P("tensor", None),
        ),
        out_specs=P(None, ("dp", "tensor")),
        check_vma=False,
    )
```

```python
import jax
import jax.numpy as jnp
from jax import lax
from jax.experimental import pallas as pl
from jax.experimental.pallas import tpu as pltpu
from jax.sharding import PartitionSpec as P

PAD_ID = 128004
DAMP = 0.1
TRAIN = 512
FEAT = 4096
MESH = pl.DeviceIdType.MESH
F32 = jnp.float32
BF16 = jnp.bfloat16


SLOT = (0, 1, 3, 5, 7, 6, 4, 2)


def kernel(
    th, tg, tids, qh, qg, qids, pin, pout, out,
    TH, TG, QH, QG, TIDS, QIDS, WI, WO,
    XQ, XT, RCQ, RCT, YQ, YT, RZQ, RZT,
    QPS, RQ1, CS, RC1, RQ2, ES, EO, EP, EH, EL, RB, SC, FR, OUT,
    hsem, cs, cr, zs, zr, q1s, q1r, q2s, q2r, es, er, fs, fr, rs, rr, osem, orem, lsem, inside,
):
    dp = lax.axis_index("dp")
    tt = lax.axis_index("tensor")
    y = lax.div(dp, 16)
    x = lax.rem(lax.div(dp, 4), 4)
    zh = lax.rem(dp, 4)
    zl = lax.div(tt, 2)
    k = lax.rem(tt, 2)
    z = zh * 2 + zl
    col = y * 4 + x
    far = 1 - zl
    mate = (dp, zl * 2 + (1 - k))
    across = (dp, far * 2 + k)
    corner = (dp, far * 2 + (1 - k))

    def column(n):
        m = lax.rem(n + 10, 16)
        return lax.rem(y + lax.div(m, 4), 4) * 4 + lax.rem(x + lax.rem(m, 4), 4)

    def level(there, step):
        nz = lax.rem(z + step, 8)
        return (there * 4 + lax.div(nz, 2), lax.rem(nz, 2) * 2 + k)

    def plane(fn):
        def body(n, carry):
            there = column(n)
            fn(there, (there * 4 + zh, tt))
            return carry

        lax.fori_loop(0, 6, body, 0)
        lax.fori_loop(7, 16, body, 0)

    def unit_loads(unit):
        pair = pl.ds((unit % 2) * 4 + (far if unit < 2 else zl) * 2, 2)
        return [
            pltpu.make_async_copy(th.at[pair], TH.at[unit], hsem.at[6 + 2 * unit]),
            pltpu.make_async_copy(tg.at[pair], TG.at[unit], hsem.at[7 + 2 * unit]),
        ]

    weights = [
        pltpu.make_async_copy(pin, WI.at[0:64], hsem.at[0]),
        pltpu.make_async_copy(pout, WO.at[64:128], hsem.at[1]),
    ]
    units = [unit_loads(unit) for unit in range(4)]
    query = [
        pltpu.make_async_copy(qh, QH, hsem.at[2]),
        pltpu.make_async_copy(qg, QG, hsem.at[3]),
    ]
    ids = [
        pltpu.make_async_copy(qids, QIDS, hsem.at[4]),
        pltpu.make_async_copy(tids, TIDS, hsem.at[5]),
    ]
    for load in weights + units[0]:
        load.start()

    barrier = pltpu.get_barrier_semaphore()

    def greet(device):
        pl.semaphore_signal(barrier, inc=1, device_id=device, device_id_type=MESH)

    plane(lambda there, device: greet(device))
    for step in range(1, 8):
        greet(level(col, step))
    greet(mate)
    greet(corner)

    for load in units[1] + query + units[2] + units[3] + ids:
        load.start()

    def remote(src, dst, send, recv, device):
        return pltpu.make_async_remote_copy(
            src_ref=src, dst_ref=dst, send_sem=send, recv_sem=recv,
            device_id=device, device_id_type=MESH,
        )

    def drain(ref, sem):
        pltpu.make_async_copy(ref, ref, sem).wait()

    def project(hidden, grads):
        dims = (((1,), (1,)), ((), ()))
        return lax.dot_general(hidden, WI[...], dims, preferred_element_type=F32) + lax.dot_general(
            grads, WO[...], dims, preferred_element_type=F32
        )

    WI[64:128] = jnp.zeros_like(WI[64:128])
    WO[0:64] = jnp.zeros_like(WO[0:64])
    def train_unit(unit):
        for load in units[unit]:
            load.wait()
        for half in range(2):
            XT[unit, half] = project(TH[unit, half], TG[unit, half])

    for load in weights:
        load.wait()
    train_unit(0)
    train_unit(1)
    for load in query:
        load.wait()
    for half in range(2):
        rows = slice(half * 8, half * 8 + 8)
        XQ[half] = project(QH[rows].reshape(128, -1), QG[rows].reshape(128, -1)).reshape(2, 64, 128)

    pl.semaphore_wait(barrier, 24)
    core = [remote(XT.at[u, 1 - k], RCT.at[u], cs.at[u], cr.at[u], mate) for u in range(4)]
    core_q = remote(XQ.at[:, 1 - k], RCQ, cs.at[4], cr.at[4], mate)
    for copy in [core_q] + core[:2]:
        copy.start()
    for step in range(1, 8):
        pl.semaphore_signal(inside, inc=1, device_id=level(col, step), device_id_type=MESH)

    core_q.wait_recv()
    YQ[...] = XQ[:, k] + RCQ[...]
    cross_q = remote(YQ.at[far], RZQ, zs.at[2], zr.at[2], across)
    cross_q.start()
    cross = []
    for u in range(2):
        core[u].wait_recv()
        YT[u] = XT[u, k] + RCT[u]
        copy = remote(YT.at[u], RZT.at[u], zs.at[u], zr.at[u], across)
        copy.start()
        cross.append(copy)
    for u in range(2, 4):
        train_unit(u)
        core[u].start()

    lane = lax.broadcasted_iota(jnp.int32, (32, 128), 1)

    def pack(both):
        return jnp.where(lane < 64, pltpu.roll(both[0:32], 64, 1), both[32:64])

    ids[0].wait()
    cross_q.wait_recv()
    side = YQ[zl] + RZQ[...]
    mask = (QIDS[pl.ds(tt * 4, 4), :] != PAD_ID).astype(F32)
    CS[...] = jnp.broadcast_to(jnp.sum(mask, axis=1, keepdims=True), (4, 128))
    wide = jnp.concatenate([mask] * 4, axis=1)
    owner = lax.div(lax.broadcasted_iota(jnp.int32, (4, 64), 1), 16)
    wide = jnp.where(owner == lax.broadcasted_iota(jnp.int32, (4, 64), 0), wide, 0.0)
    turned = side.T[0:64]
    masked = jnp.concatenate([turned * wide[q : q + 1] for q in range(4)], axis=0)
    both = jnp.dot(masked, side, precision=lax.Precision.HIGHEST, preferred_element_type=F32)
    for q in range(4):
        packed = pack(both[q * 64 : q * 64 + 64])
        for f in range(2):
            QPS[pl.ds(f * 4 + q, 16, stride=8), :] = packed[f * 16 : f * 16 + 16]

    def send_q1(there, device):
        remote(QPS.at[pl.ds(there * 8, 8)], RQ1.at[col], q1s.at[0], q1r.at[0], device).start()
        remote(CS, RC1.at[col], q1s.at[1], q1r.at[1], device).start()

    plane(send_q1)
    own_q = pltpu.make_async_copy(QPS.at[pl.ds(col * 8, 8)], RQ1.at[col], lsem.at[0])
    own_q.start()
    RC1[col] = CS[...]

    def send_features(chunk, there, steps):
        for step in steps:
            slot = SLOT[step]
            remote(
                ES.at[chunk, pl.ds(there * 2, 2)], EO.at[slot, pl.ds(col * 4 + chunk * 2, 2)],
                es.at[slot], er.at[slot], level(there, step),
            ).start()

    ids[1].wait()
    owns = []
    for chunk in range(2):
        core[2 + chunk].wait_recv()
        cross[chunk].wait_recv()
        tokens = XT[2 + chunk, k] + RCT[2 + chunk] + RZT[chunk]
        mask = (TIDS[pl.ds(chunk * 4 + tt, 1), :] != PAD_ID).astype(F32)
        both = jnp.dot(
            tokens.T[0:64] * mask, tokens,
            precision=lax.Precision.HIGHEST, preferred_element_type=F32,
        )
        packed = pack(both) / jnp.sum(mask, axis=1, keepdims=True)
        for f in range(2):
            ES[chunk, pl.ds(f, 16, stride=2), :] = packed[f * 16 : f * 16 + 16]
        if chunk == 0:
            pl.semaphore_wait(inside, 7)

        def features(n, carry, chunk=chunk):
            send_features(chunk, column(n), (4, 5, 3, 6, 2, 7, 1, 0))
            return carry

        lax.fori_loop(0, 6, features, 0)
        lax.fori_loop(7, 16, features, 0)
        send_features(chunk, col, (4, 5, 3, 6, 2, 7, 1))
        own = pltpu.make_async_copy(
            ES.at[chunk, pl.ds(col * 2, 2)], EO.at[0, pl.ds(col * 4 + chunk * 2, 2)], lsem.at[1 + chunk]
        )
        own.start()
        owns.append(own)

    own_q.wait()
    drain(RQ1.at[pl.ds(0, 15)], q1r.at[0])
    drain(RC1.at[pl.ds(0, 15)], q1r.at[1])
    RQ2[zh, 0:8] = jnp.sum(RQ1[...], axis=0)
    RQ2[zh, 8:12] = jnp.sum(RC1[...], axis=0)
    for n in range(1, 4):
        device = (col * 4 + lax.rem(zh + n, 4), tt)
        remote(RQ2.at[zh], RQ2.at[zh], q2s, q2r, device).start()

    squares = jnp.zeros((16, 128), F32)

    def halves(ref, slot, at, squares):
        for part in range(4):
            chunk, f = part // 2, part % 2
            block = ref[slot, pl.ds(part, 16, stride=4), :]
            squares = squares + block * block
            high = block.astype(BF16)
            rows = slice(at + slot * 32 + chunk * 16, at + slot * 32 + chunk * 16 + 16)
            EH[rows, f * 128 : f * 128 + 128] = high
            EL[rows, f * 128 : f * 128 + 128] = (block - high.astype(F32)).astype(BF16)
        return squares

    for own in owns:
        own.wait()
    forwards = []
    for slot in range(8):
        drain(EO.at[slot, pl.ds(0, 60 if slot == 0 else 64)], er.at[slot])
        copy = remote(EO.at[slot], EP.at[slot], fs.at[slot], fr.at[slot], mate)
        copy.start()
        forwards.append(copy)
        squares = halves(EO, slot, 0, squares)
    for slot in range(8):
        forwards[slot].wait_recv()
        squares = halves(EP, slot, 256, squares)

    drain(RQ2.at[pl.ds(0, 3)], q2r)
    total = jnp.sum(RQ2[...], axis=0)
    queries = jnp.concatenate([total[0:4], total[4:8]], axis=1) / total[8:12, 0:1]

    def stacked(v):
        high = v.astype(BF16).astype(F32)
        return jnp.concatenate([high, v - high], axis=0).astype(BF16)

    def product(v, contract):
        v = stacked(v)
        dims = (((1,), (contract,)), ((), ()))
        whole = lax.dot_general(v, EH[...], dims, preferred_element_type=F32) + lax.dot_general(
            v, EL[...], dims, preferred_element_type=F32
        )
        return whole[0:4] + whole[4:8]

    spot = lax.broadcasted_iota(jnp.int32, (4, 128), 1)

    def share(step, partial_value, first, second):
        for b in range(4):
            RB[step, col, b] = partial_value[:, b * 128 : b * 128 + 128]
        RB[step, col, 4] = jnp.where(spot == 0, first, jnp.where(spot == 1, second, 0.0))

        def send(there, device):
            remote(RB.at[step, col], RB.at[step, col], rs.at[step], rr.at[step], device).start()

        plane(send)
        drain(RB.at[step, pl.ds(0, 15)], rr.at[step])
        whole = jnp.sum(RB[step], axis=0)
        return (
            jnp.concatenate([whole[b] for b in range(4)], axis=1),
            whole[4][:, 0:1],
            whole[4][:, 1:2],
        )

    def rowsum(v):
        return jnp.sum(v, axis=1, keepdims=True)

    residual = direction = queries
    trace = jnp.sum(jnp.sum(squares, axis=0, keepdims=True), axis=1, keepdims=True)
    seen, norm_now, trace = share(0, product(residual, 1), rowsum(residual * residual), trace)
    scale = TRAIN * (DAMP * (trace / TRAIN) / FEAT)
    length = norm_now
    scores = None
    for step in range(3):
        alpha = norm_now / (length + rowsum(seen * seen) / scale)
        scores = alpha * seen if step == 0 else scores + alpha * seen
        if step == 2:
            break
        image = direction + product(seen, 0) / scale
        residual = residual - alpha * image
        fresh_seen, fresh, along = share(
            step + 1, product(residual, 1), rowsum(residual * residual), rowsum(residual * direction)
        )
        beta = fresh / norm_now
        seen = fresh_seen + beta * seen
        length = fresh + 2.0 * beta * along + beta * beta * length
        direction = residual + beta * direction
        norm_now = fresh

    for h in range(2):
        SC[h] = scores[:, h * 256 : h * 256 + 128]
    for n, device in enumerate((mate, across, corner)):
        for p in range(2):
            remote(
                SC.at[lax.rem(p + k, 2)], FR.at[p, pl.ds(tt * 4, 4)], osem.at[n], orem.at[n * 2 + p], device
            ).start()
    mine = [
        pltpu.make_async_copy(SC.at[lax.rem(p + k, 2)], FR.at[p, pl.ds(tt * 4, 4)], lsem.at[3 + p])
        for p in range(2)
    ]
    for copy in mine:
        copy.start()
    group = lax.rem(lax.div(lax.broadcasted_iota(jnp.int32, (32, 128), 0), 4), 4)
    place = jnp.where(group < 2, k * 64, (1 - k) * 32) + zl * 16 + col
    place = lax.broadcasted_iota(jnp.int32, (32, 128), 1) == place
    for copy in mine:
        copy.wait()
    for n in range(6):
        drain(FR.at[0, pl.ds(0, 4)], orem.at[n])
    picked = jnp.where(place, FR[...].reshape(32, 128), 0.0)
    turned = lax.dot_general(
        jnp.ones((8, 128), F32), picked, (((1,), (1,)), ((), ())),
        precision=lax.Precision.HIGHEST, preferred_element_type=F32,
    )
    OUT[0:1] = turned[0:1, 0:16]
    OUT[1:2] = turned[0:1, 16:32]
    result = pltpu.make_async_copy(OUT, out, lsem.at[5])
    result.start()

    core_q.wait_send()
    cross_q.wait_send()
    for copy in core + cross + forwards:
        copy.wait_send()
    drain(RQ1.at[pl.ds(0, 15)], q1s.at[0])
    drain(RC1.at[pl.ds(0, 15)], q1s.at[1])
    drain(RQ2.at[pl.ds(0, 3)], q2s)
    for slot in range(8):
        drain(EO.at[slot, pl.ds(0, 60 if slot == 0 else 64)], es.at[slot])
    for step in range(3):
        drain(RB.at[step, pl.ds(0, 15)], rs.at[step])
    for n in range(3):
        drain(FR.at[0, pl.ds(0, 8)], osem.at[n])
    result.wait()


def per_device(th, tg, tids, qh, qg, qids, pin, pout):
    V = pltpu.VMEM
    D = pltpu.SemaphoreType.DMA
    scores = pl.pallas_call(
        kernel,
        out_shape=jax.ShapeDtypeStruct((2, 16), F32),
        in_specs=[pl.BlockSpec(memory_space=pl.ANY)] * 8,
        out_specs=pl.BlockSpec(memory_space=pl.ANY),
        scratch_shapes=[
            V((4, 2) + th.shape[1:], BF16), V((4, 2) + tg.shape[1:], BF16), V(qh.shape, BF16), V(qg.shape, BF16),
            V(tids.shape, jnp.int32), V(qids.shape, jnp.int32),
            V((128, pin.shape[0]), BF16), V((128, pout.shape[0]), BF16),
            V((2, 2, 64, 128), F32), V((4, 2, 128, 128), F32),
            V((2, 64, 128), F32), V((4, 128, 128), F32),
            V((2, 64, 128), F32), V((2, 128, 128), F32),
            V((64, 128), F32), V((2, 128, 128), F32),
            V((128, 128), F32), V((16, 8, 128), F32),
            V((4, 128), F32), V((16, 4, 128), F32),
            V((4, 12, 128), F32),
            V((2, 32, 128), F32), V((8, 64, 128), F32), V((8, 64, 128), F32),
            V((512, 256), BF16), V((512, 256), BF16),
            V((3, 16, 5, 4, 128), F32),
            V((2, 4, 128), F32), V((2, 16, 128), F32), V((2, 16), F32),
            D((14,)), D((5,)), D((5,)), D((3,)), D((3,)), D((2,)), D((2,)), D, D,
            D((8,)), D((8,)), D((8,)), D((8,)), D((3,)), D((3,)), D((3,)), D((6,)), D((6,)),
            pltpu.SemaphoreType.REGULAR,
        ],
        compiler_params=pltpu.CompilerParams(
            collective_id=0, has_side_effects=True, vmem_limit_bytes=56 * 1024 * 1024
        ),
        cost_estimate=pl.CostEstimate(flops=10**9, bytes_accessed=13 * 10**6, transcendentals=0),
    )(th, tg, tids, qh, qg, qids, pin.T, pout.T)
    return scores.T


def solution(mesh):
    return jax.shard_map(
        per_device,
        mesh=mesh,
        in_specs=(
            P("dp", None, "tensor"),
            P("dp", None, "tensor"),
            P("dp", None),
            P(None, "dp", "tensor"),
            P(None, "dp", "tensor"),
            P(None, "dp"),
            P("tensor", None),
            P("tensor", None),
        ),
        out_specs=P(None, ("dp", "tensor")),
        check_vma=False,
    )
```

```python
import jax
import jax.numpy as jnp
from jax import lax
from jax.experimental import pallas as pl
from jax.experimental.pallas import tpu as pltpu
from jax.sharding import PartitionSpec as P

PAD_ID = 128004
DAMP = 0.1
TRAIN = 512
FEAT = 4096
MESH = pl.DeviceIdType.MESH
F32 = jnp.float32
BF16 = jnp.bfloat16


SLOT = (0, 1, 3, 5, 7, 6, 4, 2)


def kernel(
    th, tg, tids, qh, qg, qids, pin, pout, out,
    TH, TG, QH, QG, TIDS, QIDS, WI, WO,
    XQ, XT, RCQ, RCT, YQ, YT, RZQ, RZT,
    QPS, RQ1, RQ2, ES, EO, EP, EH, EL, RB, SC, FR,
    hsem, cs, cr, zs, zr, q1s, q1r, q2s, q2r, es, er, fs, fr, rs, rr, osem, orem, lsem, inside,
):
    dp = lax.axis_index("dp")
    tt = lax.axis_index("tensor")
    y = lax.div(dp, 16)
    x = lax.rem(lax.div(dp, 4), 4)
    zh = lax.rem(dp, 4)
    zl = lax.div(tt, 2)
    k = lax.rem(tt, 2)
    z = zh * 2 + zl
    col = y * 4 + x
    far = 1 - zl
    mate = (dp, zl * 2 + (1 - k))
    across = (dp, far * 2 + k)
    corner = (dp, far * 2 + (1 - k))

    def column(n):
        m = lax.rem(n + 10, 16)
        return lax.rem(y + lax.div(m, 4), 4) * 4 + lax.rem(x + lax.rem(m, 4), 4)

    floors = [lax.rem(z + step, 8) for step in range(8)]
    floors = [(lax.div(nz, 2), lax.rem(nz, 2) * 2 + k) for nz in floors]

    def level(there, step):
        return (there * 4 + floors[step][0], floors[step][1])

    def plane(fn):
        def body(n, carry):
            there = column(n)
            fn(there, (there * 4 + zh, tt))
            return carry

        lax.fori_loop(0, 6, body, 0)
        lax.fori_loop(7, 16, body, 0)

    def unit_loads(unit):
        pair = pl.ds((unit % 2) * 4 + (far if unit < 2 else zl) * 2, 2)
        return [
            pltpu.make_async_copy(th.at[pair], TH.at[unit], hsem.at[6 + 2 * unit]),
            pltpu.make_async_copy(tg.at[pair], TG.at[unit], hsem.at[7 + 2 * unit]),
        ]

    weights = [
        pltpu.make_async_copy(pin, WI.at[0:64], hsem.at[0]),
        pltpu.make_async_copy(pout, WO.at[64:128], hsem.at[1]),
    ]
    units = [unit_loads(unit) for unit in range(4)]
    query = [
        pltpu.make_async_copy(qh, QH, hsem.at[2]),
        pltpu.make_async_copy(qg, QG, hsem.at[3]),
    ]
    ids = [
        pltpu.make_async_copy(qids, QIDS, hsem.at[4]),
        pltpu.make_async_copy(tids, TIDS, hsem.at[5]),
    ]
    for load in weights + query:
        load.start()

    barrier = pltpu.get_barrier_semaphore()

    def greet(device):
        pl.semaphore_signal(barrier, inc=1, device_id=device, device_id_type=MESH)

    plane(lambda there, device: greet(device))
    for step in range(1, 8):
        greet(level(col, step))
    greet(mate)
    greet(corner)

    for load in units[0] + units[1] + units[2] + units[3] + ids:
        load.start()

    def remote(src, dst, send, recv, device):
        return pltpu.make_async_remote_copy(
            src_ref=src, dst_ref=dst, send_sem=send, recv_sem=recv,
            device_id=device, device_id_type=MESH,
        )

    def drain(ref, sem):
        pltpu.make_async_copy(ref, ref, sem).wait()

    def project(hidden, grads):
        dims = (((1,), (1,)), ((), ()))
        return lax.dot_general(hidden, WI[...], dims, preferred_element_type=F32) + lax.dot_general(
            grads, WO[...], dims, preferred_element_type=F32
        )

    WI[64:128] = jnp.zeros_like(WI[64:128])
    WO[0:64] = jnp.zeros_like(WO[0:64])
    def train_unit(unit):
        for load in units[unit]:
            load.wait()
        for half in range(2):
            XT[unit, half] = project(TH[unit, half], TG[unit, half])

    for load in weights + query:
        load.wait()
    for half in range(2):
        rows = slice(half * 8, half * 8 + 8)
        XQ[half] = project(QH[rows].reshape(128, -1), QG[rows].reshape(128, -1)).reshape(2, 64, 128)

    pl.semaphore_wait(barrier, 24)
    core = [remote(XT.at[u, 1 - k], RCT.at[u], cs.at[u], cr.at[u], mate) for u in range(4)]
    cross = [remote(YT.at[u], RZT.at[u], zs.at[u], zr.at[u], across) for u in range(2)]
    core_q = remote(XQ.at[:, 1 - k], RCQ, cs.at[4], cr.at[4], mate)
    cross_q = remote(YQ.at[far], RZQ, zs.at[2], zr.at[2], across)
    core_q.start()
    for step in range(1, 8):
        pl.semaphore_signal(inside, inc=1, device_id=level(col, step), device_id_type=MESH)

    def pass_on(u):
        core[u].wait_recv()
        YT[u] = XT[u, k] + RCT[u]
        cross[u].start()

    train_unit(0)
    core[0].start()
    core_q.wait_recv()
    YQ[...] = XQ[:, k] + RCQ[...]
    cross_q.start()
    train_unit(1)
    core[1].start()
    pass_on(0)
    train_unit(2)
    core[2].start()
    pass_on(1)
    train_unit(3)
    core[3].start()

    lane = lax.broadcasted_iota(jnp.int32, (32, 128), 1)

    def pack(both):
        return jnp.where(lane < 64, pltpu.roll(both[0:32], 64, 1), both[32:64])

    ids[0].wait()
    cross_q.wait_recv()
    side = YQ[zl] + RZQ[...]
    mask = (QIDS[pl.ds(tt * 4, 4), :] != PAD_ID).astype(F32)
    count = jnp.broadcast_to(jnp.sum(mask, axis=1, keepdims=True), (4, 128))
    wide = jnp.concatenate([mask] * 4, axis=1)
    owner = lax.div(lax.broadcasted_iota(jnp.int32, (4, 64), 1), 16)
    wide = jnp.where(owner == lax.broadcasted_iota(jnp.int32, (4, 64), 0), wide, 0.0)
    turned = side.T[0:64]
    masked = jnp.concatenate([turned * wide[q : q + 1] for q in range(4)], axis=0)
    both = jnp.dot(masked, side, precision=lax.Precision.HIGHEST, preferred_element_type=F32)
    for q in range(4):
        packed = pack(both[q * 64 : q * 64 + 64])
        for f in range(2):
            QPS[pl.ds(f * 4 + q, 16, stride=12), :] = packed[f * 16 : f * 16 + 16]

    for c in range(16):
        QPS[c * 12 + 8 : c * 12 + 12, :] = count

    def send_q1(there, device):
        remote(QPS.at[pl.ds(there * 12, 12)], RQ1.at[col], q1s, q1r, device).start()

    plane(send_q1)
    own_q = pltpu.make_async_copy(QPS.at[pl.ds(col * 12, 12)], RQ1.at[col], lsem.at[0])
    own_q.start()

    def send_features(chunk, there, steps):
        for step in steps:
            slot = SLOT[step]
            remote(
                ES.at[chunk, pl.ds(there * 2, 2)], EO.at[slot, pl.ds(col * 4 + chunk * 2, 2)],
                es.at[slot], er.at[slot], level(there, step),
            ).start()

    ids[1].wait()
    owns = []
    for chunk in range(2):
        core[2 + chunk].wait_recv()
        cross[chunk].wait_recv()
        tokens = XT[2 + chunk, k] + RCT[2 + chunk] + RZT[chunk]
        mask = (TIDS[pl.ds(chunk * 4 + tt, 1), :] != PAD_ID).astype(F32)
        both = jnp.dot(
            tokens.T[0:64] * mask, tokens,
            precision=lax.Precision.HIGHEST, preferred_element_type=F32,
        )
        packed = pack(both) / jnp.sum(mask, axis=1, keepdims=True)
        for f in range(2):
            ES[chunk, pl.ds(f, 16, stride=2), :] = packed[f * 16 : f * 16 + 16]
        if chunk == 0:
            pl.semaphore_wait(inside, 7)

        def features(n, carry, chunk=chunk):
            send_features(chunk, column(n), (4, 5, 3, 6, 2, 7, 1, 0))
            return carry

        lax.fori_loop(0, 6, features, 0)
        lax.fori_loop(7, 16, features, 0)
        send_features(chunk, col, (4, 5, 3, 6, 2, 7, 1))
        own = pltpu.make_async_copy(
            ES.at[chunk, pl.ds(col * 2, 2)], EO.at[0, pl.ds(col * 4 + chunk * 2, 2)], lsem.at[1 + chunk]
        )
        own.start()
        owns.append(own)

    own_q.wait()
    drain(RQ1.at[pl.ds(0, 15)], q1r)
    RQ2[zh] = jnp.sum(RQ1[...], axis=0)
    for n in range(1, 4):
        device = (col * 4 + lax.rem(zh + n, 4), tt)
        remote(RQ2.at[zh], RQ2.at[zh], q2s, q2r, device).start()

    squares = jnp.zeros((16, 128), F32)

    def halves(ref, slot, at, squares):
        for part in range(4):
            chunk, f = part // 2, part % 2
            block = ref[slot, pl.ds(part, 16, stride=4), :]
            squares = squares + block * block
            high = block.astype(BF16)
            rows = slice(at + slot * 32 + chunk * 16, at + slot * 32 + chunk * 16 + 16)
            EH[rows, f * 128 : f * 128 + 128] = high
            EL[rows, f * 128 : f * 128 + 128] = (block - high.astype(F32)).astype(BF16)
        return squares

    for own in owns:
        own.wait()
    forwards = []
    for slot in range(8):
        drain(EO.at[slot, pl.ds(0, 60 if slot == 0 else 64)], er.at[slot])
        copy = remote(EO.at[slot], EP.at[slot], fs.at[slot], fr.at[slot], mate)
        copy.start()
        forwards.append(copy)
        squares = halves(EO, slot, 0, squares)
    for slot in range(8):
        forwards[slot].wait_recv()
        squares = halves(EP, slot, 256, squares)

    drain(RQ2.at[pl.ds(0, 3)], q2r)
    total = jnp.sum(RQ2[...], axis=0)
    queries = jnp.concatenate([total[0:4], total[4:8]], axis=1) / total[8:12, 0:1]

    def stacked(v):
        high = v.astype(BF16).astype(F32)
        return jnp.concatenate([high, v - high], axis=0).astype(BF16)

    def product(v, contract):
        v = stacked(v)
        dims = (((1,), (contract,)), ((), ()))
        whole = lax.dot_general(v, EH[...], dims, preferred_element_type=F32) + lax.dot_general(
            v, EL[...], dims, preferred_element_type=F32
        )
        return whole[0:4] + whole[4:8]

    spot = lax.broadcasted_iota(jnp.int32, (4, 128), 1)

    def share(step, partial_value, first, second):
        for b in range(4):
            RB[step, col, b] = partial_value[:, b * 128 : b * 128 + 128]
        RB[step, col, 4] = jnp.where(spot == 0, first, jnp.where(spot == 1, second, 0.0))

        def send(there, device):
            remote(RB.at[step, col], RB.at[step, col], rs.at[step], rr.at[step], device).start()

        plane(send)
        drain(RB.at[step, pl.ds(0, 15)], rr.at[step])
        whole = jnp.sum(RB[step], axis=0)
        return (
            jnp.concatenate([whole[b] for b in range(4)], axis=1),
            whole[4][:, 0:1],
            whole[4][:, 1:2],
        )

    def rowsum(v):
        return jnp.sum(v, axis=1, keepdims=True)

    residual = direction = queries
    trace = jnp.sum(jnp.sum(squares, axis=0, keepdims=True), axis=1, keepdims=True)
    seen, norm_now, trace = share(0, product(residual, 1), rowsum(residual * residual), trace)
    scale = TRAIN * (DAMP * (trace / TRAIN) / FEAT)
    length = norm_now
    scores = None
    for step in range(3):
        alpha = norm_now / (length + rowsum(seen * seen) / scale)
        scores = alpha * seen if step == 0 else scores + alpha * seen
        if step == 2:
            break
        image = direction + product(seen, 0) / scale
        residual = residual - alpha * image
        fresh_seen, fresh, along = share(
            step + 1, product(residual, 1), rowsum(residual * residual), rowsum(residual * direction)
        )
        beta = fresh / norm_now
        seen = fresh_seen + beta * seen
        length = fresh + 2.0 * beta * along + beta * beta * length
        direction = residual + beta * direction
        norm_now = fresh

    for h in range(2):
        SC[h] = scores[:, h * 256 : h * 256 + 128]
    for n, device in enumerate((mate, across, corner)):
        for p in range(2):
            remote(
                SC.at[lax.rem(p + k, 2)], FR.at[p, pl.ds(tt * 4, 4)], osem.at[n], orem.at[n * 2 + p], device
            ).start()
    mine = [
        pltpu.make_async_copy(SC.at[lax.rem(p + k, 2)], FR.at[p, pl.ds(tt * 4, 4)], lsem.at[3 + p])
        for p in range(2)
    ]
    for copy in mine:
        copy.start()
    group = lax.rem(lax.div(lax.broadcasted_iota(jnp.int32, (32, 128), 0), 4), 4)
    place = jnp.where(group < 2, k * 64, (1 - k) * 32) + zl * 16 + col
    place = lax.broadcasted_iota(jnp.int32, (32, 128), 1) == place
    for copy in mine:
        copy.wait()
    for n in range(6):
        drain(FR.at[0, pl.ds(0, 4)], orem.at[n])
    picked = jnp.where(place, FR[...].reshape(32, 128), 0.0)
    turned = lax.dot_general(
        jnp.ones((8, 128), F32), picked, (((1,), (1,)), ((), ())),
        precision=lax.Precision.HIGHEST, preferred_element_type=F32,
    )
    out[0:1] = turned[0:1, 0:16]
    out[1:2] = turned[0:1, 16:32]

    core_q.wait_send()
    cross_q.wait_send()
    for copy in core + cross + forwards:
        copy.wait_send()
    drain(RQ1.at[pl.ds(0, 15)], q1s)
    drain(RQ2.at[pl.ds(0, 3)], q2s)
    for slot in range(8):
        drain(EO.at[slot, pl.ds(0, 60 if slot == 0 else 64)], es.at[slot])
    for step in range(3):
        drain(RB.at[step, pl.ds(0, 15)], rs.at[step])
    for n in range(3):
        drain(FR.at[0, pl.ds(0, 8)], osem.at[n])


def per_device(th, tg, tids, qh, qg, qids, pin, pout):
    V = pltpu.VMEM
    D = pltpu.SemaphoreType.DMA
    scores = pl.pallas_call(
        kernel,
        out_shape=pltpu.VMEM((2, 16), F32),
        in_specs=[pl.BlockSpec(memory_space=pl.ANY)] * 8,
        out_specs=pl.BlockSpec(memory_space=pltpu.VMEM),
        scratch_shapes=[
            V((4, 2) + th.shape[1:], BF16), V((4, 2) + tg.shape[1:], BF16), V(qh.shape, BF16), V(qg.shape, BF16),
            V(tids.shape, jnp.int32), V(qids.shape, jnp.int32),
            V((128, pin.shape[0]), BF16), V((128, pout.shape[0]), BF16),
            V((2, 2, 64, 128), F32), V((4, 2, 128, 128), F32),
            V((2, 64, 128), F32), V((4, 128, 128), F32),
            V((2, 64, 128), F32), V((2, 128, 128), F32),
            V((64, 128), F32), V((2, 128, 128), F32),
            V((192, 128), F32), V((16, 12, 128), F32),
            V((4, 12, 128), F32),
            V((2, 32, 128), F32), V((8, 64, 128), F32), V((8, 64, 128), F32),
            V((512, 256), BF16), V((512, 256), BF16),
            V((3, 16, 5, 4, 128), F32),
            V((2, 4, 128), F32), V((2, 16, 128), F32),
            D((14,)), D((5,)), D((5,)), D((3,)), D((3,)), D, D, D, D,
            D((8,)), D((8,)), D((8,)), D((8,)), D((3,)), D((3,)), D((3,)), D((6,)), D((5,)),
            pltpu.SemaphoreType.REGULAR,
        ],
        compiler_params=pltpu.CompilerParams(
            collective_id=0, has_side_effects=True, vmem_limit_bytes=56 * 1024 * 1024
        ),
        cost_estimate=pl.CostEstimate(flops=10**9, bytes_accessed=13 * 10**6, transcendentals=0),
    )(th, tg, tids, qh, qg, qids, pin.T, pout.T)
    return scores.T


def solution(mesh):
    return jax.shard_map(
        per_device,
        mesh=mesh,
        in_specs=(
            P("dp", None, "tensor"),
            P("dp", None, "tensor"),
            P("dp", None),
            P(None, "dp", "tensor"),
            P(None, "dp", "tensor"),
            P(None, "dp"),
            P("tensor", None),
            P("tensor", None),
        ),
        out_specs=P(None, ("dp", "tensor")),
        check_vma=False,
    )
```

```python
import jax
import jax.numpy as jnp
from jax import lax
from jax.experimental import pallas as pl
from jax.experimental.pallas import tpu as pltpu
from jax.sharding import PartitionSpec as P

PAD_ID = 128004
DAMP = 0.1
TRAIN = 512
FEAT = 4096
MESH = pl.DeviceIdType.MESH
F32 = jnp.float32
BF16 = jnp.bfloat16


SLOT = (0, 1, 3, 5, 7, 6, 4, 2)


def kernel(
    th, tg, tids, qh, qg, qids, pin, pout, out,
    TH, TG, QH, QG, TIDS, QIDS, WI, WO,
    XQ, XT, RCQ, RCT, YQ, YT, RZQ, RZT,
    QPS, RQ1, RQ2, ES, EO, EP, EH, EL, RB, SC, FR,
    hsem, cs, cr, zs, zr, q1s, q1r, q2s, q2r, es, er, fs, fr, rs, rr, osem, orem, lsem, inside,
):
    dp = lax.axis_index("dp")
    tt = lax.axis_index("tensor")
    y = lax.div(dp, 16)
    x = lax.rem(lax.div(dp, 4), 4)
    zh = lax.rem(dp, 4)
    zl = lax.div(tt, 2)
    k = lax.rem(tt, 2)
    z = zh * 2 + zl
    col = y * 4 + x
    far = 1 - zl
    mate = (dp, zl * 2 + (1 - k))
    across = (dp, far * 2 + k)
    corner = (dp, far * 2 + (1 - k))

    def column(n):
        m = lax.rem(n + 10, 16)
        return lax.rem(y + lax.div(m, 4), 4) * 4 + lax.rem(x + lax.rem(m, 4), 4)

    floors = [lax.rem(z + step, 8) for step in range(8)]
    floors = [(lax.div(nz, 2), lax.rem(nz, 2) * 2 + k) for nz in floors]

    def level(there, step):
        return (there * 4 + floors[step][0], floors[step][1])

    columns = [column(n) for n in range(16) if n != 6]

    def plane(fn):
        for there in columns:
            fn(there, (there * 4 + zh, tt))

    def unit_loads(unit):
        pair = pl.ds((unit % 2) * 4 + (far if unit < 2 else zl) * 2, 2)
        return [
            pltpu.make_async_copy(th.at[pair], TH.at[unit], hsem.at[6 + 2 * unit]),
            pltpu.make_async_copy(tg.at[pair], TG.at[unit], hsem.at[7 + 2 * unit]),
        ]

    weights = [
        pltpu.make_async_copy(pin, WI.at[0:64], hsem.at[0]),
        pltpu.make_async_copy(pout, WO.at[64:128], hsem.at[1]),
    ]
    units = [unit_loads(unit) for unit in range(4)]
    query = [
        pltpu.make_async_copy(qh, QH, hsem.at[2]),
        pltpu.make_async_copy(qg, QG, hsem.at[3]),
    ]
    ids = [
        pltpu.make_async_copy(qids, QIDS, hsem.at[4]),
        pltpu.make_async_copy(tids, TIDS, hsem.at[5]),
    ]
    for load in weights + query:
        load.start()

    barrier = pltpu.get_barrier_semaphore()

    def greet(device):
        pl.semaphore_signal(barrier, inc=1, device_id=device, device_id_type=MESH)

    plane(lambda there, device: greet(device))
    for step in range(1, 8):
        greet(level(col, step))
    greet(mate)
    greet(corner)

    for load in units[0] + units[1] + units[2] + units[3] + ids:
        load.start()

    def remote(src, dst, send, recv, device):
        return pltpu.make_async_remote_copy(
            src_ref=src, dst_ref=dst, send_sem=send, recv_sem=recv,
            device_id=device, device_id_type=MESH,
        )

    def drain(ref, sem):
        pltpu.make_async_copy(ref, ref, sem).wait()

    def project(hidden, grads):
        dims = (((1,), (1,)), ((), ()))
        return lax.dot_general(hidden, WI[...], dims, preferred_element_type=F32) + lax.dot_general(
            grads, WO[...], dims, preferred_element_type=F32
        )

    WI[64:128] = jnp.zeros_like(WI[64:128])
    WO[0:64] = jnp.zeros_like(WO[0:64])
    def train_unit(unit):
        for load in units[unit]:
            load.wait()
        for half in range(2):
            XT[unit, half] = project(TH[unit, half], TG[unit, half])

    for load in weights + query:
        load.wait()
    for half in range(2):
        rows = slice(half * 8, half * 8 + 8)
        XQ[half] = project(QH[rows].reshape(128, -1), QG[rows].reshape(128, -1)).reshape(2, 64, 128)

    pl.semaphore_wait(barrier, 24)
    core = [remote(XT.at[u, 1 - k], RCT.at[u], cs.at[0], cr.at[u], mate) for u in range(4)]
    cross = [remote(YT.at[u], RZT.at[u], zs.at[u], zr.at[u], across) for u in range(2)]
    core_q = remote(XQ.at[:, 1 - k], RCQ, cs.at[1], cr.at[4], mate)
    cross_q = remote(YQ.at[far], RZQ, zs.at[2], zr.at[2], across)
    core_q.start()
    for step in range(1, 8):
        pl.semaphore_signal(inside, inc=1, device_id=level(col, step), device_id_type=MESH)

    def pass_on(u):
        core[u].wait_recv()
        YT[u] = XT[u, k] + RCT[u]
        cross[u].start()

    train_unit(0)
    core[0].start()
    core_q.wait_recv()
    YQ[...] = XQ[:, k] + RCQ[...]
    cross_q.start()
    train_unit(1)
    core[1].start()
    pass_on(0)
    train_unit(2)
    core[2].start()
    pass_on(1)
    train_unit(3)
    core[3].start()

    lane = lax.broadcasted_iota(jnp.int32, (32, 128), 1)

    def pack(both):
        return jnp.where(lane < 64, pltpu.roll(both[0:32], 64, 1), both[32:64])

    ids[0].wait()
    cross_q.wait_recv()
    side = YQ[zl] + RZQ[...]
    mask = (QIDS[pl.ds(tt * 4, 4), :] != PAD_ID).astype(F32)
    count = jnp.broadcast_to(jnp.sum(mask, axis=1, keepdims=True), (4, 128))
    wide = jnp.concatenate([mask] * 4, axis=1)
    owner = lax.div(lax.broadcasted_iota(jnp.int32, (4, 64), 1), 16)
    wide = jnp.where(owner == lax.broadcasted_iota(jnp.int32, (4, 64), 0), wide, 0.0)
    turned = side.T[0:64]
    masked = jnp.concatenate([turned * wide[q : q + 1] for q in range(4)], axis=0)
    both = jnp.dot(masked, side, precision=lax.Precision.HIGHEST, preferred_element_type=F32)
    for q in range(4):
        packed = pack(both[q * 64 : q * 64 + 64])
        for f in range(2):
            QPS[pl.ds(f * 4 + q, 16, stride=12), :] = packed[f * 16 : f * 16 + 16]

    for c in range(16):
        QPS[c * 12 + 8 : c * 12 + 12, :] = count

    def send_q1(there, device):
        remote(QPS.at[pl.ds(there * 12, 12)], RQ1.at[col], q1s, q1r, device).start()

    plane(send_q1)
    own_q = pltpu.make_async_copy(QPS.at[pl.ds(col * 12, 12)], RQ1.at[col], lsem.at[0])
    own_q.start()

    def send_features(chunk, there, steps):
        for step in steps:
            slot = SLOT[step]
            remote(
                ES.at[chunk, pl.ds(there * 2, 2)], EO.at[slot, pl.ds(col * 4 + chunk * 2, 2)],
                es, er.at[slot], level(there, step),
            ).start()

    ids[1].wait()
    owns = []
    for chunk in range(2):
        core[2 + chunk].wait_recv()
        cross[chunk].wait_recv()
        tokens = XT[2 + chunk, k] + RCT[2 + chunk] + RZT[chunk]
        mask = (TIDS[pl.ds(chunk * 4 + tt, 1), :] != PAD_ID).astype(F32)
        both = jnp.dot(
            tokens.T[0:64] * mask, tokens,
            precision=lax.Precision.HIGHEST, preferred_element_type=F32,
        )
        packed = pack(both) / jnp.sum(mask, axis=1, keepdims=True)
        for f in range(2):
            ES[chunk, pl.ds(f, 16, stride=2), :] = packed[f * 16 : f * 16 + 16]
        if chunk == 0:
            pl.semaphore_wait(inside, 7)

        def features(n, carry, chunk=chunk):
            send_features(chunk, column(n), (4, 5, 3, 6, 2, 7, 1, 0))
            return carry

        lax.fori_loop(0, 6, features, 0)
        lax.fori_loop(7, 16, features, 0)
        send_features(chunk, col, (4, 5, 3, 6, 2, 7, 1))
        own = pltpu.make_async_copy(
            ES.at[chunk, pl.ds(col * 2, 2)], EO.at[0, pl.ds(col * 4 + chunk * 2, 2)], lsem.at[1 + chunk]
        )
        own.start()
        owns.append(own)

    own_q.wait()
    drain(RQ1.at[pl.ds(0, 15)], q1r)
    RQ2[zh] = jnp.sum(RQ1[...], axis=0)
    for n in range(1, 4):
        device = (col * 4 + lax.rem(zh + n, 4), tt)
        remote(RQ2.at[zh], RQ2.at[zh], q2s, q2r, device).start()

    squares = jnp.zeros((16, 128), F32)

    def halves(ref, slot, at, squares):
        for part in range(4):
            chunk, f = part // 2, part % 2
            block = ref[slot, pl.ds(part, 16, stride=4), :]
            squares = squares + block * block
            high = block.astype(BF16)
            rows = slice(at + slot * 32 + chunk * 16, at + slot * 32 + chunk * 16 + 16)
            EH[rows, f * 128 : f * 128 + 128] = high
            EL[rows, f * 128 : f * 128 + 128] = (block - high.astype(F32)).astype(BF16)
        return squares

    for own in owns:
        own.wait()
    forwards = []
    for slot in range(8):
        drain(EO.at[slot, pl.ds(0, 60 if slot == 0 else 64)], er.at[slot])
        copy = remote(EO.at[slot], EP.at[slot], fs, fr.at[slot], mate)
        copy.start()
        forwards.append(copy)
        squares = halves(EO, slot, 0, squares)
    for slot in range(8):
        forwards[slot].wait_recv()
        squares = halves(EP, slot, 256, squares)

    drain(RQ2.at[pl.ds(0, 3)], q2r)
    total = jnp.sum(RQ2[...], axis=0)
    queries = jnp.concatenate([total[0:4], total[4:8]], axis=1) / total[8:12, 0:1]

    def stacked(v):
        high = v.astype(BF16).astype(F32)
        return jnp.concatenate([high, v - high], axis=0).astype(BF16)

    def product(v, contract):
        v = stacked(v)
        dims = (((1,), (contract,)), ((), ()))
        whole = lax.dot_general(v, EH[...], dims, preferred_element_type=F32) + lax.dot_general(
            v, EL[...], dims, preferred_element_type=F32
        )
        return whole[0:4] + whole[4:8]

    spot = lax.broadcasted_iota(jnp.int32, (4, 128), 1)

    def share(step, partial_value, first, second):
        for b in range(4):
            RB[step, col, b] = partial_value[:, b * 128 : b * 128 + 128]
        RB[step, col, 4] = jnp.where(spot == 0, first, jnp.where(spot == 1, second, 0.0))

        def send(there, device):
            remote(RB.at[step, col], RB.at[step, col], rs, rr.at[step], device).start()

        plane(send)
        drain(RB.at[step, pl.ds(0, 15)], rr.at[step])
        whole = jnp.sum(RB[step], axis=0)
        return (
            jnp.concatenate([whole[b] for b in range(4)], axis=1),
            whole[4][:, 0:1],
            whole[4][:, 1:2],
        )

    def rowsum(v):
        return jnp.sum(v, axis=1, keepdims=True)

    residual = direction = queries
    trace = jnp.sum(jnp.sum(squares, axis=0, keepdims=True), axis=1, keepdims=True)
    seen, norm_now, trace = share(0, product(residual, 1), rowsum(residual * residual), trace)
    scale = TRAIN * (DAMP * (trace / TRAIN) / FEAT)
    length = norm_now
    scores = None
    for step in range(3):
        alpha = norm_now / (length + rowsum(seen * seen) / scale)
        scores = alpha * seen if step == 0 else scores + alpha * seen
        if step == 2:
            break
        image = direction + product(seen, 0) / scale
        residual = residual - alpha * image
        fresh_seen, fresh, along = share(
            step + 1, product(residual, 1), rowsum(residual * residual), rowsum(residual * direction)
        )
        beta = fresh / norm_now
        seen = fresh_seen + beta * seen
        length = fresh + 2.0 * beta * along + beta * beta * length
        direction = residual + beta * direction
        norm_now = fresh

    for h in range(2):
        SC[h] = scores[:, h * 256 : h * 256 + 128]
    for n, device in enumerate((mate, across, corner)):
        for p in range(2):
            remote(
                SC.at[lax.rem(p + k, 2)], FR.at[p, pl.ds(tt * 4, 4)], osem, orem.at[n * 2 + p], device
            ).start()
    mine = [
        pltpu.make_async_copy(SC.at[lax.rem(p + k, 2)], FR.at[p, pl.ds(tt * 4, 4)], lsem.at[3 + p])
        for p in range(2)
    ]
    for copy in mine:
        copy.start()
    group = lax.rem(lax.div(lax.broadcasted_iota(jnp.int32, (32, 128), 0), 4), 4)
    place = jnp.where(group < 2, k * 64, (1 - k) * 32) + zl * 16 + col
    place = lax.broadcasted_iota(jnp.int32, (32, 128), 1) == place
    for copy in mine:
        copy.wait()
    for n in range(6):
        drain(FR.at[0, pl.ds(0, 4)], orem.at[n])
    picked = jnp.where(place, FR[...].reshape(32, 128), 0.0)
    turned = lax.dot_general(
        jnp.ones((8, 128), F32), picked, (((1,), (1,)), ((), ())),
        precision=lax.Precision.HIGHEST, preferred_element_type=F32,
    )
    out[0:1] = turned[0:1, 0:16]
    out[1:2] = turned[0:1, 16:32]

    core_q.wait_send()
    cross_q.wait_send()
    for copy in cross:
        copy.wait_send()
    drain(RCT, cs.at[0])
    drain(EO, fs)
    drain(RQ1.at[pl.ds(0, 15)], q1s)
    drain(RQ2.at[pl.ds(0, 3)], q2s)
    drain(XT.at[:, 0, pl.ds(0, 127)], es)
    drain(RB.at[:, pl.ds(0, 15)], rs)
    drain(FR.at[:, pl.ds(0, 12)], osem)


def per_device(th, tg, tids, qh, qg, qids, pin, pout):
    V = pltpu.VMEM
    D = pltpu.SemaphoreType.DMA
    scores = pl.pallas_call(
        kernel,
        out_shape=pltpu.VMEM((2, 16), F32),
        in_specs=[pl.BlockSpec(memory_space=pl.ANY)] * 8,
        out_specs=pl.BlockSpec(memory_space=pltpu.VMEM),
        scratch_shapes=[
            V((4, 2) + th.shape[1:], BF16), V((4, 2) + tg.shape[1:], BF16), V(qh.shape, BF16), V(qg.shape, BF16),
            V(tids.shape, jnp.int32), V(qids.shape, jnp.int32),
            V((128, pin.shape[0]), BF16), V((128, pout.shape[0]), BF16),
            V((2, 2, 64, 128), F32), V((4, 2, 128, 128), F32),
            V((2, 64, 128), F32), V((4, 128, 128), F32),
            V((2, 64, 128), F32), V((2, 128, 128), F32),
            V((64, 128), F32), V((2, 128, 128), F32),
            V((192, 128), F32), V((16, 12, 128), F32),
            V((4, 12, 128), F32),
            V((2, 32, 128), F32), V((8, 64, 128), F32), V((8, 64, 128), F32),
            V((512, 256), BF16), V((512, 256), BF16),
            V((3, 16, 5, 4, 128), F32),
            V((2, 4, 128), F32), V((2, 16, 128), F32),
            D((14,)), D((2,)), D((5,)), D((3,)), D((3,)), D, D, D, D,
            D, D((8,)), D, D((8,)), D, D((3,)), D, D((6,)), D((5,)),
            pltpu.SemaphoreType.REGULAR,
        ],
        compiler_params=pltpu.CompilerParams(
            collective_id=0, has_side_effects=True, vmem_limit_bytes=56 * 1024 * 1024
        ),
        cost_estimate=pl.CostEstimate(flops=10**9, bytes_accessed=13 * 10**6, transcendentals=0),
    )(th, tg, tids, qh, qg, qids, pin.T, pout.T)
    return scores.T


def solution(mesh):
    return jax.shard_map(
        per_device,
        mesh=mesh,
        in_specs=(
            P("dp", None, "tensor"),
            P("dp", None, "tensor"),
            P("dp", None),
            P(None, "dp", "tensor"),
            P(None, "dp", "tensor"),
            P(None, "dp"),
            P("tensor", None),
            P("tensor", None),
        ),
        out_specs=P(None, ("dp", "tensor")),
        check_vma=False,
    )
```

```python
import jax
import jax.numpy as jnp
from jax import lax
from jax.experimental import pallas as pl
from jax.experimental.pallas import tpu as pltpu
from jax.sharding import PartitionSpec as P

PAD_ID = 128004
DAMP = 0.1
TRAIN = 512
FEAT = 4096
MESH = pl.DeviceIdType.MESH
F32 = jnp.float32
BF16 = jnp.bfloat16


SLOT = (0, 1, 3, 5, 7, 6, 4, 2)


def kernel(
    th, tg, tids, qh, qg, qids, pin, pout, out,
    TH, TG, QH, QG, TIDS, QIDS, WI, WO,
    XQ, XT, RCQ, RCT, YQ, YT, RZQ, RZT,
    QPS, RQ1, RQ2, ES, EO, EP, EH, EL, RB, SC, FR,
    hsem, cs, cr, zs, zr, q1s, q1r, q2s, q2r, es, er, fs, fr, rs, rr, osem, orem, lsem, inside,
):
    dp = lax.axis_index("dp")
    tt = lax.axis_index("tensor")
    y = lax.div(dp, 16)
    x = lax.rem(lax.div(dp, 4), 4)
    zh = lax.rem(dp, 4)
    zl = lax.div(tt, 2)
    k = lax.rem(tt, 2)
    z = zh * 2 + zl
    col = y * 4 + x
    far = 1 - zl
    mate = (dp, zl * 2 + (1 - k))
    across = (dp, far * 2 + k)
    corner = (dp, far * 2 + (1 - k))

    def column(n):
        m = lax.rem(n + 10, 16)
        return lax.rem(y + lax.div(m, 4), 4) * 4 + lax.rem(x + lax.rem(m, 4), 4)

    floors = [lax.rem(z + step, 8) for step in range(8)]
    floors = [(lax.div(nz, 2), lax.rem(nz, 2) * 2 + k) for nz in floors]

    def level(there, step):
        return (there * 4 + floors[step][0], floors[step][1])

    columns = [column(n) for n in range(16) if n != 6]

    def plane(fn):
        for there in columns:
            fn(there, (there * 4 + zh, tt))

    def unit_loads(unit):
        pair = pl.ds((unit % 2) * 4 + (far if unit < 2 else zl) * 2, 2)
        return [
            pltpu.make_async_copy(th.at[pair], TH.at[unit], hsem.at[6 + 2 * unit]),
            pltpu.make_async_copy(tg.at[pair], TG.at[unit], hsem.at[7 + 2 * unit]),
        ]

    weights = [
        pltpu.make_async_copy(pin, WI.at[0:64], hsem.at[0]),
        pltpu.make_async_copy(pout, WO.at[64:128], hsem.at[1]),
    ]
    units = [unit_loads(unit) for unit in range(4)]
    query = [
        pltpu.make_async_copy(qh, QH, hsem.at[2]),
        pltpu.make_async_copy(qg, QG, hsem.at[3]),
    ]
    ids = [
        pltpu.make_async_copy(qids, QIDS, hsem.at[4]),
        pltpu.make_async_copy(tids, TIDS, hsem.at[5]),
    ]
    for load in weights + query:
        load.start()

    barrier = pltpu.get_barrier_semaphore()

    def greet(device):
        pl.semaphore_signal(barrier, inc=1, device_id=device, device_id_type=MESH)

    plane(lambda there, device: greet(device))
    for step in range(1, 8):
        greet(level(col, step))
    greet(mate)
    greet(corner)

    for load in units[0] + units[1] + units[2] + units[3] + ids:
        load.start()

    def remote(src, dst, send, recv, device):
        return pltpu.make_async_remote_copy(
            src_ref=src, dst_ref=dst, send_sem=send, recv_sem=recv,
            device_id=device, device_id_type=MESH,
        )

    def drain(ref, sem):
        pltpu.make_async_copy(ref, ref, sem).wait()

    def project(hidden, grads):
        dims = (((1,), (1,)), ((), ()))
        return lax.dot_general(hidden, WI[...], dims, preferred_element_type=F32) + lax.dot_general(
            grads, WO[...], dims, preferred_element_type=F32
        )

    WI[64:128] = jnp.zeros_like(WI[64:128])
    WO[0:64] = jnp.zeros_like(WO[0:64])
    def train_unit(unit):
        for load in units[unit]:
            load.wait()
        for half in range(2):
            XT[unit, half] = project(TH[unit, half], TG[unit, half])

    for load in weights + query:
        load.wait()
    for half in range(2):
        rows = slice(half * 8, half * 8 + 8)
        XQ[half] = project(QH[rows].reshape(128, -1), QG[rows].reshape(128, -1)).reshape(2, 64, 128)

    pl.semaphore_wait(barrier, 24)
    core = [remote(XT.at[u, 1 - k], RCT.at[u], cs.at[0], cr.at[u], mate) for u in range(4)]
    cross = [remote(YT.at[u], RZT.at[u], zs.at[u], zr.at[u], across) for u in range(2)]
    core_q = remote(XQ.at[:, 1 - k], RCQ, cs.at[1], cr.at[4], mate)
    cross_q = remote(YQ.at[far], RZQ, zs.at[2], zr.at[2], across)
    core_q.start()
    for step in range(1, 8):
        pl.semaphore_signal(inside, inc=1, device_id=level(col, step), device_id_type=MESH)

    def pass_on(u):
        core[u].wait_recv()
        YT[u] = XT[u, k] + RCT[u]
        cross[u].start()

    train_unit(0)
    core[0].start()
    core_q.wait_recv()
    YQ[...] = XQ[:, k] + RCQ[...]
    cross_q.start()
    train_unit(1)
    core[1].start()
    pass_on(0)
    train_unit(2)
    core[2].start()
    pass_on(1)
    train_unit(3)
    core[3].start()

    lane = lax.broadcasted_iota(jnp.int32, (32, 128), 1)

    def pack(both):
        return jnp.where(lane < 64, pltpu.roll(both[0:32], 64, 1), both[32:64])

    ids[0].wait()
    cross_q.wait_recv()
    side = YQ[zl] + RZQ[...]
    mask = (QIDS[pl.ds(tt * 4, 4), :] != PAD_ID).astype(F32)
    count = jnp.broadcast_to(jnp.sum(mask, axis=1, keepdims=True), (4, 128))
    wide = jnp.concatenate([mask] * 4, axis=1)
    owner = lax.div(lax.broadcasted_iota(jnp.int32, (4, 64), 1), 16)
    wide = jnp.where(owner == lax.broadcasted_iota(jnp.int32, (4, 64), 0), wide, 0.0)
    turned = side.T[0:64]
    masked = jnp.concatenate([turned * wide[q : q + 1] for q in range(4)], axis=0)
    both = jnp.dot(masked, side, precision=lax.Precision.HIGHEST, preferred_element_type=F32)
    for q in range(4):
        packed = pack(both[q * 64 : q * 64 + 64])
        for f in range(2):
            QPS[pl.ds(f * 4 + q, 16, stride=12), :] = packed[f * 16 : f * 16 + 16]

    for c in range(16):
        QPS[c * 12 + 8 : c * 12 + 12, :] = count

    def send_q1(there, device):
        remote(QPS.at[pl.ds(there * 12, 12)], RQ1.at[col], q1s, q1r, device).start()

    plane(send_q1)
    own_q = pltpu.make_async_copy(QPS.at[pl.ds(col * 12, 12)], RQ1.at[col], lsem.at[0])
    own_q.start()

    def send_features(chunk, there, steps):
        for step in steps:
            slot = SLOT[step]
            remote(
                ES.at[chunk, pl.ds(there * 2, 2)], EO.at[slot, pl.ds(col * 4 + chunk * 2, 2)],
                es, er.at[slot], level(there, step),
            ).start()

    ids[1].wait()
    owns = []
    for chunk in range(2):
        core[2 + chunk].wait_recv()
        cross[chunk].wait_recv()
        tokens = XT[2 + chunk, k] + RCT[2 + chunk] + RZT[chunk]
        mask = (TIDS[pl.ds(chunk * 4 + tt, 1), :] != PAD_ID).astype(F32)
        both = jnp.dot(
            tokens.T[0:64] * mask, tokens,
            precision=lax.Precision.HIGHEST, preferred_element_type=F32,
        )
        packed = pack(both) / jnp.sum(mask, axis=1, keepdims=True)
        for f in range(2):
            ES[chunk, pl.ds(f, 16, stride=2), :] = packed[f * 16 : f * 16 + 16]
        if chunk == 0:
            pl.semaphore_wait(inside, 7)

        def features(n, carry, chunk=chunk):
            send_features(chunk, column(n), (4, 5, 3, 6, 2, 7, 1, 0))
            return carry

        lax.fori_loop(0, 6, features, 0)
        lax.fori_loop(7, 16, features, 0)
        send_features(chunk, col, (4, 5, 3, 6, 2, 7, 1))
        own = pltpu.make_async_copy(
            ES.at[chunk, pl.ds(col * 2, 2)], EO.at[0, pl.ds(col * 4 + chunk * 2, 2)], lsem.at[1 + chunk]
        )
        own.start()
        owns.append(own)

    own_q.wait()
    drain(RQ1.at[pl.ds(0, 15)], q1r)
    RQ2[zh] = jnp.sum(RQ1[...], axis=0)
    for n in range(1, 4):
        device = (col * 4 + lax.rem(zh + n, 4), tt)
        remote(RQ2.at[zh], RQ2.at[zh], q2s, q2r, device).start()

    squares = jnp.zeros((16, 128), F32)

    def halves(ref, slot, at, squares):
        for part in range(4):
            chunk, f = part // 2, part % 2
            block = ref[slot, pl.ds(part, 16, stride=4), :]
            squares = squares + block * block
            high = block.astype(BF16)
            rows = slice(at + slot * 32 + chunk * 16, at + slot * 32 + chunk * 16 + 16)
            EH[rows, f * 128 : f * 128 + 128] = high
            EL[rows, f * 128 : f * 128 + 128] = (block - high.astype(F32)).astype(BF16)
        return squares

    for own in owns:
        own.wait()
    forwards = []
    for slot in range(8):
        drain(EO.at[slot, pl.ds(0, 60 if slot == 0 else 64)], er.at[slot])
        copy = remote(EO.at[slot], EP.at[slot], fs, fr.at[slot], mate)
        copy.start()
        forwards.append(copy)
        squares = halves(EO, slot, 0, squares)
    for slot in range(8):
        forwards[slot].wait_recv()
        squares = halves(EP, slot, 256, squares)

    drain(RQ2.at[pl.ds(0, 3)], q2r)
    total = jnp.sum(RQ2[...], axis=0)
    queries = jnp.concatenate([total[0:4], total[4:8]], axis=1) / total[8:12, 0:1]

    def stacked(v):
        high = v.astype(BF16).astype(F32)
        return jnp.concatenate([high, v - high], axis=0).astype(BF16)

    def product(v, contract):
        v = stacked(v)
        dims = (((1,), (contract,)), ((), ()))
        parts = []
        for n in range(2):
            at = (slice(n * 256, n * 256 + 256), slice(0, 256)) if contract else (slice(0, 512), slice(n * 128, n * 128 + 128))
            parts.append(
                lax.dot_general(v, EH[at], dims, preferred_element_type=F32)
                + lax.dot_general(v, EL[at], dims, preferred_element_type=F32)
            )
        whole = jnp.concatenate(parts, axis=1)
        return whole[0:4] + whole[4:8]

    spot = lax.broadcasted_iota(jnp.int32, (4, 128), 1)

    def share(step, partial_value, first, second):
        for b in range(4):
            RB[step, col, b] = partial_value[:, b * 128 : b * 128 + 128]
        RB[step, col, 4] = jnp.where(spot == 0, first, jnp.where(spot == 1, second, 0.0))

        def send(there, device):
            remote(RB.at[step, col], RB.at[step, col], rs, rr.at[step], device).start()

        plane(send)
        drain(RB.at[step, pl.ds(0, 15)], rr.at[step])
        whole = jnp.sum(RB[step], axis=0)
        return (
            jnp.concatenate([whole[b] for b in range(4)], axis=1),
            whole[4][:, 0:1],
            whole[4][:, 1:2],
        )

    def rowsum(v):
        return jnp.sum(v, axis=1, keepdims=True)

    residual = direction = queries
    trace = jnp.sum(jnp.sum(squares, axis=0, keepdims=True), axis=1, keepdims=True)
    seen, norm_now, trace = share(0, product(residual, 1), rowsum(residual * residual), trace)
    scale = TRAIN * (DAMP * (trace / TRAIN) / FEAT)
    length = norm_now
    scores = None
    for step in range(3):
        alpha = norm_now / (length + rowsum(seen * seen) / scale)
        scores = alpha * seen if step == 0 else scores + alpha * seen
        if step == 2:
            break
        image = direction + product(seen, 0) / scale
        residual = residual - alpha * image
        fresh_seen, fresh, along = share(
            step + 1, product(residual, 1), rowsum(residual * residual), rowsum(residual * direction)
        )
        beta = fresh / norm_now
        seen = fresh_seen + beta * seen
        length = fresh + 2.0 * beta * along + beta * beta * length
        direction = residual + beta * direction
        norm_now = fresh

    for h in range(2):
        SC[h] = scores[:, h * 256 : h * 256 + 128]
    for n, device in enumerate((mate, across, corner)):
        for p in range(2):
            remote(
                SC.at[lax.rem(p + k, 2)], FR.at[p, pl.ds(tt * 4, 4)], osem, orem.at[n * 2 + p], device
            ).start()
    mine = [
        pltpu.make_async_copy(SC.at[lax.rem(p + k, 2)], FR.at[p, pl.ds(tt * 4, 4)], lsem.at[3 + p])
        for p in range(2)
    ]
    for copy in mine:
        copy.start()
    group = lax.rem(lax.div(lax.broadcasted_iota(jnp.int32, (32, 128), 0), 4), 4)
    place = jnp.where(group < 2, k * 64, (1 - k) * 32) + zl * 16 + col
    place = lax.broadcasted_iota(jnp.int32, (32, 128), 1) == place
    for copy in mine:
        copy.wait()
    for n in range(6):
        drain(FR.at[0, pl.ds(0, 4)], orem.at[n])
    picked = jnp.where(place, FR[...].reshape(32, 128), 0.0)
    turned = lax.dot_general(
        jnp.ones((8, 128), F32), picked, (((1,), (1,)), ((), ())),
        precision=lax.Precision.HIGHEST, preferred_element_type=F32,
    )
    out[0:1] = turned[0:1, 0:16]
    out[1:2] = turned[0:1, 16:32]

    core_q.wait_send()
    cross_q.wait_send()
    for copy in cross:
        copy.wait_send()
    drain(RCT, cs.at[0])
    drain(EO, fs)
    drain(RQ1.at[pl.ds(0, 15)], q1s)
    drain(RQ2.at[pl.ds(0, 3)], q2s)
    drain(XT.at[:, 0, pl.ds(0, 127)], es)
    drain(RB.at[:, pl.ds(0, 15)], rs)
    drain(FR.at[:, pl.ds(0, 12)], osem)


def per_device(th, tg, tids, qh, qg, qids, pin, pout):
    V = pltpu.VMEM
    D = pltpu.SemaphoreType.DMA
    scores = pl.pallas_call(
        kernel,
        out_shape=pltpu.VMEM((2, 16), F32),
        in_specs=[pl.BlockSpec(memory_space=pl.ANY)] * 8,
        out_specs=pl.BlockSpec(memory_space=pltpu.VMEM),
        scratch_shapes=[
            V((4, 2) + th.shape[1:], BF16), V((4, 2) + tg.shape[1:], BF16), V(qh.shape, BF16), V(qg.shape, BF16),
            V(tids.shape, jnp.int32), V(qids.shape, jnp.int32),
            V((128, pin.shape[0]), BF16), V((128, pout.shape[0]), BF16),
            V((2, 2, 64, 128), F32), V((4, 2, 128, 128), F32),
            V((2, 64, 128), F32), V((4, 128, 128), F32),
            V((2, 64, 128), F32), V((2, 128, 128), F32),
            V((64, 128), F32), V((2, 128, 128), F32),
            V((192, 128), F32), V((16, 12, 128), F32),
            V((4, 12, 128), F32),
            V((2, 32, 128), F32), V((8, 64, 128), F32), V((8, 64, 128), F32),
            V((512, 256), BF16), V((512, 256), BF16),
            V((3, 16, 5, 4, 128), F32),
            V((2, 4, 128), F32), V((2, 16, 128), F32),
            D((14,)), D((2,)), D((5,)), D((3,)), D((3,)), D, D, D, D,
            D, D((8,)), D, D((8,)), D, D((3,)), D, D((6,)), D((5,)),
            pltpu.SemaphoreType.REGULAR,
        ],
        compiler_params=pltpu.CompilerParams(
            collective_id=0, has_side_effects=True, vmem_limit_bytes=56 * 1024 * 1024
        ),
        cost_estimate=pl.CostEstimate(flops=10**9, bytes_accessed=13 * 10**6, transcendentals=0),
    )(th, tg, tids, qh, qg, qids, pin.T, pout.T)
    return scores.T


def solution(mesh):
    return jax.shard_map(
        per_device,
        mesh=mesh,
        in_specs=(
            P("dp", None, "tensor"),
            P("dp", None, "tensor"),
            P("dp", None),
            P(None, "dp", "tensor"),
            P(None, "dp", "tensor"),
            P(None, "dp"),
            P("tensor", None),
            P("tensor", None),
        ),
        out_specs=P(None, ("dp", "tensor")),
        check_vma=False,
    )
```
